512 devices in a mesh: slab: 8 (over y_hi, x), tile: 64 (over z, y_lo, core).
Axes of the slice: x: 4, y: 4 (y_hi: 2, y_lo: 2; y = y_hi * 2 + y_lo), z: 16, core: 2. Of those that a mesh axis runs over, the one named last changes fastest.
Arguments:
- source: float32 [16, 2, 3, 128, 64, 128], P(None, None, None, 'tile', 'slab'), may hold values from -48 to 48
- soil_index: int32 [128, 64, 128], P('tile', 'slab'), may hold values from 0 to 7
- soil_table: float32 [3, 8], replicated, may hold values from 0.5 to 2
- pml_width: int32 [8, 2], P('slab'), may hold values from 1 to 4
- interface_blocks: float32 [128, 8, 2, 384, 384], P('tile', 'slab'), may hold values from -0.25 to 0.25
- inflow: float32 [128, 2, 16, 384], P('tile'), may hold values from -6 to 6
Outputs:
- solution: float32 [16, 2, 3, 128, 64, 128], P(None, None, None, 'tile', 'slab')
- traces: float32 [128, 8, 2, 16, 384], P('tile', 'slab')
The draws below stay inside these ranges and needn't reach their ends.
All inputs are finite; a program needn't handle non-finite values.
Results may differ from the reference program's by a relative error of at most 0.0001.
Values sent between devices are 32-bit elements; how exact they have to be, the bound alone decides.
No kernel may reach another device: no remote copies, remote signals or barrier semaphores. Data moves between devices by JAX's collectives and lax.ppermute only.
A program may use at most 128 MiB of HBM per device.

```python
import math
import jax
import jax.numpy as jnp
from jax import lax

NRHS = 16
NY = 128
DZ = 8
ITERS = 3
PATCH = 64
LAYERS = 8
SLABS = 8
NX = 128
NZ = 64
NP = 2
BLOCK = 384


def set_ends(array, stream_key, least, largest):
    shape = array.shape
    place = [jax.random.randint(jax.random.fold_in(stream_key, axis), (), 0, shape[axis]) for axis in range(len(shape))]
    array = array.at[tuple(place)].set(least)
    longest = shape.index(max(shape))
    place[longest] = (place[longest] + 1) % shape[longest]
    return array.at[tuple(place)].set(largest)


def levels(own_key, dims, split, smallest, top_value):
    gain = 1.0
    for dim, shards_of in split:
        draws = jax.random.uniform(jax.random.fold_in(jax.random.fold_in(own_key, 6), dim), (shards_of,), jnp.float32, smallest / len(split), top_value / len(split))
        gain = gain * jnp.repeat(jnp.exp(draws), dims[dim] // shards_of).reshape((-1,) + (1,) * (len(dims) - 1 - dim))
    return gain


def noise(stream_key, dims, deviation, reach, split=(), kind=jnp.bfloat16):
    gain = levels(stream_key, dims, split, -0.22, 0.18) if split else 1.0
    values = jax.random.normal(stream_key, dims, jnp.float32) * deviation * gain
    return jnp.minimum(jnp.maximum(values, -reach), reach).astype(kind)


def setup_inputs(seed: int = 0) -> dict:
    arg_keys = jax.random.split(jax.random.key(seed), 7)
    return {
        "source": noise(arg_keys[0], (NRHS, 2, 3, NX, NZ, NY), 8.0, 48.0, ((3, 64), (4, 8)), jnp.float32),
        "soil_index": set_ends(jax.random.randint(arg_keys[1], (NX, NZ, NY), 0, LAYERS), jax.random.fold_in(arg_keys[1], 1), 0, LAYERS - 1).astype(jnp.int32),
        "soil_table": jnp.clip(jnp.exp(jax.random.uniform(arg_keys[2], (3, LAYERS), jnp.float32, math.log(0.5), math.log(2.0))), 0.5, 2.0),
        "pml_width": set_ends(jax.random.randint(arg_keys[3], (SLABS, 2), 1, DZ // 2 + 1), jax.random.fold_in(arg_keys[3], 1), 1, (DZ // 2 + 1) - 1).astype(jnp.int32),
        "interface_blocks": noise(arg_keys[4], (NX, SLABS, NP, BLOCK, BLOCK), (0.9 / (6 * PATCH) ** 0.5), 0.25, ((0, 64), (1, 8)), jnp.float32),
        "inflow": noise(arg_keys[5], (NX, NP, NRHS, BLOCK), 1.0, 6.0, ((0, 64),), jnp.float32),
    }


RELAX_WEIGHT = 0.8
SIGMA_PEAK = 3.0
UNIT_STEPS = ((1, 0, 0), (0, 0, 1), (0, 1, 0))


def neighbour(padded, offset, component):
    width_cells = padded.shape[3] - 2
    depth_cells = padded.shape[4] - 2
    length_cells = padded.shape[5] - 2
    return padded[:, :, component, 1 + offset[0]:1 + offset[0] + width_cells, 1 + offset[1]:1 + offset[1] + depth_cells, 1 + offset[2]:1 + offset[2] + length_cells]


def negate(offset):
    return tuple(-entry for entry in offset)


def joined(first_off, second_off, sign_factor):
    return tuple(first_entry + sign_factor * second_entry for first_entry, second_entry in zip(first_off, second_off))


def stiffness(padded, shear_mod, lame_first):
    every_comp = slice(None)
    centre = neighbour(padded, (0, 0, 0), every_comp)
    face_sum = neighbour(padded, (1, 0, 0), every_comp) + neighbour(padded, (-1, 0, 0), every_comp)
    face_sum = face_sum + neighbour(padded, (0, 1, 0), every_comp) + neighbour(padded, (0, -1, 0), every_comp)
    face_sum = face_sum + neighbour(padded, (0, 0, 1), every_comp) + neighbour(padded, (0, 0, -1), every_comp)
    laplace_term = 6.0 * centre - face_sum
    term_list = []
    for component in range(3):
        own_step = UNIT_STEPS[component]
        own_term = 2.0 * centre[:, :, component] - neighbour(padded, own_step, component) - neighbour(padded, negate(own_step), component)
        for other_dir in range(3):
            if other_dir != component:
                plus_step = joined(own_step, UNIT_STEPS[other_dir], 1)
                minus_step = joined(own_step, UNIT_STEPS[other_dir], -1)
                cross_term = neighbour(padded, plus_step, other_dir) + neighbour(padded, negate(plus_step), other_dir)
                cross_term = cross_term - neighbour(padded, minus_step, other_dir) - neighbour(padded, negate(minus_step), other_dir)
                own_term = own_term - 0.25 * cross_term
        term_list.append(own_term)
    grad_term = jnp.stack(term_list, axis=2)
    return shear_mod * laplace_term + (lame_first + shear_mod) * grad_term


def relax_step(field_now, padded, source_field, coeffs):
    shear_mod, lame_first, mass_term, damp_rate = coeffs
    stiff_part = stiffness(padded, shear_mod, lame_first)
    real_part = field_now[:, 0]
    imag_part = field_now[:, 1]
    res_real = source_field[:, 0] - stiff_part[:, 0] - mass_term * (real_part - damp_rate * imag_part)
    res_imag = source_field[:, 1] - stiff_part[:, 1] - mass_term * (imag_part + damp_rate * real_part)
    diag_real = 6.0 * shear_mod + 2.0 * (lame_first + shear_mod) + mass_term
    diag_imag = mass_term * damp_rate
    step_scale = RELAX_WEIGHT / (diag_real * diag_real + diag_imag * diag_imag)
    new_real = real_part + step_scale * (diag_real * res_real + diag_imag * res_imag)
    new_imag = imag_part + step_scale * (diag_real * res_imag - diag_imag * res_real)
    return jnp.stack([new_real, new_imag], axis=1)


def soil_lookup(soil_index, soil_table):
    picked_list = []
    for table_row in range(3):
        picked = jnp.zeros(soil_index.shape, jnp.float32)
        for layer_id in range(soil_table.shape[1]):
            picked = picked + jnp.where(soil_index == layer_id, soil_table[table_row, layer_id], 0.0)
        picked_list.append(picked)
    return picked_list[0], picked_list[1], picked_list[2]


def damping(widths, depth_cells):
    depth_level = jnp.arange(depth_cells, dtype=jnp.int32)
    upper_damp = jnp.maximum(widths[0] - depth_level, 0).astype(jnp.float32) / widths[0].astype(jnp.float32)
    lower_damp = jnp.maximum(widths[1] - (depth_cells - 1 - depth_level), 0).astype(jnp.float32) / widths[1].astype(jnp.float32)
    return (SIGMA_PEAK * upper_damp * upper_damp + SIGMA_PEAK * lower_damp * lower_damp).reshape(1, depth_cells, 1)


def pack_plane(plane_field, patch_cells):
    shot_count, _, _, width_cells, length_cells = plane_field.shape
    block_count = length_cells // patch_cells
    grouped = plane_field.reshape(shot_count, 2, 3, width_cells, block_count, patch_cells)
    return grouped.transpose(3, 4, 0, 1, 2, 5).reshape(width_cells, block_count, shot_count, 6 * patch_cells)


def unpack_plane(vectors, patch_cells):
    width_cells, block_count, shot_count, _ = vectors.shape
    grouped = vectors.reshape(width_cells, block_count, shot_count, 2, 3, patch_cells)
    return grouped.transpose(2, 3, 4, 0, 1, 5).reshape(shot_count, 2, 3, width_cells, block_count * patch_cells)


def slab_solve(source_field, coeffs):
    field_now = jnp.zeros_like(source_field)
    for sweep_step in range(ITERS):
        padded = jnp.pad(field_now, ((0, 0), (0, 0), (0, 0), (1, 1), (1, 1), (1, 1)))
        field_now = relax_step(field_now, padded, source_field, coeffs)
    return field_now


def reference(source, soil_index, soil_table, pml_width, interface_blocks, inflow):
    coeff_list = []
    bottom_list = []
    for slab_index in range(SLABS):
        start_depth = slab_index * DZ
        shear_mod, lame_first, mass_term = soil_lookup(soil_index[:, start_depth:start_depth + DZ, :], soil_table)
        damp_rate = damping(pml_width[slab_index], DZ)
        coeffs = (shear_mod, lame_first, mass_term, damp_rate)
        coeff_list.append(coeffs)
        local_field = slab_solve(source[:, :, :, :, start_depth:start_depth + DZ, :], coeffs)
        bottom_list.append(pack_plane(local_field[:, :, :, :, DZ - 1, :], PATCH))
    incoming = inflow
    incoming_list = []
    trace_list = []
    for slab_index in range(SLABS):
        incoming_list.append(incoming)
        trace_now = jnp.einsum("xpri,xpio->xpro", incoming, interface_blocks[:, slab_index], precision=lax.Precision.HIGHEST) + bottom_list[slab_index]
        trace_list.append(trace_now)
        incoming = trace_now
    solution_list = []
    for slab_index in range(SLABS):
        start_depth = slab_index * DZ
        coeffs = coeff_list[slab_index]
        source_field = source[:, :, :, :, start_depth:start_depth + DZ, :]
        injected = source_field.at[:, :, :, :, 0, :].add(coeffs[0][:, 0, :] * unpack_plane(incoming_list[slab_index], PATCH))
        solution_list.append(slab_solve(injected, coeffs))
    return jnp.concatenate(solution_list, axis=4), jnp.stack(trace_list, axis=1)
```

```python
import functools

import jax
import jax.numpy as jnp
from jax import lax
from jax.experimental import pallas as pl
import jax.experimental.pallas.tpu as pltpu
from jax.sharding import PartitionSpec as P

PATCH = 64
RELAX_WEIGHT = 0.8
SIGMA_PEAK = 3.0
PARTS, COMPS = 2, 3
PC = PARTS * COMPS
WIDTH = 2
HALO = 2
COLS = WIDTH + 2 * HALO
DEEP = 3
COEFFS = 11
WR, WI, A, AB, H, AM, ABM, HM, AP, ABP, HP = range(COEFFS)
VMEM = pl.BlockSpec(memory_space=pltpu.VMEM)
SMEM = pl.BlockSpec(memory_space=pltpu.SMEM)
LIMIT = 24 * 1024 * 1024


def call(body, outs, operands, specs=None, scratch=(), aliases=None, flops=0):
    return pl.pallas_call(
        body,
        out_shape=[jax.ShapeDtypeStruct(shape, dtype) for shape, dtype in outs],
        in_specs=specs or [VMEM] * len(operands),
        out_specs=[VMEM] * len(outs),
        scratch_shapes=list(scratch),
        input_output_aliases=aliases or {},
        compiler_params=pltpu.CompilerParams(vmem_limit_bytes=LIMIT),
        cost_estimate=pl.CostEstimate(flops=flops, bytes_accessed=1 << 20, transcendentals=0),
    )(*operands)


def pack_kernel(shots, depth, src, soil, low, high):
    stride = PC * WIDTH * depth

    def put(target, place, d, col, pc):
        rows = src[pl.ds((pc * WIDTH + col) * depth + d, shots, stride=stride), :]
        target[pl.ds(place * shots, shots), :] = rows

    first_high = depth - DEEP
    for d in range(first_high, depth):
        for col in range(WIDTH):
            for pc in range(PC):
                put(high, ((d - first_high) * WIDTH + col) * PC + pc, d, col, pc)
    high[pl.ds(DEEP * WIDTH * PC * shots, WIDTH * depth), :] = (soil[...] + 1).astype(jnp.float32)
    for d in range(first_high):
        for col in range(WIDTH):
            for pc in range(PC):
                put(low, (d * WIDTH + col) * PC + pc, d, col, pc)


def plus(*terms):
    terms = [t for t in terms if t is not None]
    return functools.reduce(lambda a, b: a + b, terms) if terms else None


def minus(a, b):
    if b is None:
        return a
    return -b if a is None else a - b


def times(c, a):
    return None if a is None else c * a


def coupling(field, coef, x, z):
    def step(c):
        return minus(field(x + 1, z, c), field(x - 1, z, c))

    def dive(col, c):
        return minus(field(col, z + 1, c), field(col, z - 1, c))

    def sides(c):
        return plus(field(x + 1, z, c), field(x - 1, z, c))

    def ends(c):
        return plus(field(x, z + 1, c), field(x, z - 1, c))

    length = 128
    results = []
    for c in range(COMPS):
        own = field(x, z, c)
        if c == 0:
            total = plus(
                times(coef(AB), sides(0)),
                times(coef(A), ends(0)),
                times(coef(H), minus(dive(x + 1, 2), dive(x - 1, 2))),
            )
            cross = step(1)
        elif c == 1:
            total = times(coef(A), plus(sides(1), ends(1)))
            cross = plus(step(0), dive(x, 2))
        else:
            total = plus(
                times(coef(A), sides(2)),
                times(coef(AB), ends(2)),
                times(coef(H), minus(dive(x + 1, 0), dive(x - 1, 0))),
            )
            cross = dive(x, 1)
        before, after = (ABM, ABP) if c == 1 else (AM, AP)
        ahead = plus(times(coef(before), own), times(coef(HM), cross))
        behind = minus(times(coef(after), own), times(coef(HP), cross))
        if ahead is not None:
            total = plus(total, pltpu.roll(ahead, length - 1, 1), pltpu.roll(behind, 1, 1))
        results.append(total)
    return results


def relaxed(field, first, coef, x, z):
    real = coupling(lambda i, k, c: field(i, k, c), coef, x, z)
    imag = coupling(lambda i, k, c: field(i, k, COMPS + c), coef, x, z)
    wr, wi = coef(WR), coef(WI)
    out = []
    for part in range(PARTS):
        for c in range(COMPS):
            pc = part * COMPS + c
            if part == 0:
                update = minus(times(wr, real[c]), times(wi, imag[c]))
            else:
                update = plus(times(wr, imag[c]), times(wi, real[c]))
            out.append(plus(times(1.0 - RELAX_WEIGHT, field(x, z, pc)), first(x, z, pc), update))
    return out


def scaled(fr, fi, coef):
    wr, wi = coef(WR), coef(WI)
    return wr * fr - wi * fi, wr * fi + wi * fr


def memo(fn):
    cache = {}

    def get(*key):
        if key not in cache:
            cache[key] = fn(*key)
        return cache[key]

    return get


def coef_of(coeffs, col, depth, z):
    return memo(lambda j: coeffs[pl.ds((col * COEFFS + j) * depth + z, 1), :])


def rolled_zero(x, shift):
    lane = lax.broadcasted_iota(jnp.int32, x.shape, 1)
    length = x.shape[1]
    if shift == 1:
        return jnp.where(lane == 0, 0.0, pltpu.roll(x, 1, 1))
    return jnp.where(lane == length - 1, 0.0, pltpu.roll(x, length - 1, 1))


def fill_coeffs(coeffs, soils, table, widths, depth, layers):
    shape = soils[0].shape
    level = lax.broadcasted_iota(jnp.int32, shape, 0)
    top, bottom = widths[0, 0], widths[0, 1]
    zero = jnp.zeros(shape, jnp.int32)
    upper = jnp.maximum(top - level, 0).astype(jnp.float32) / (zero + top).astype(jnp.float32)
    lower = jnp.maximum(bottom - (depth - 1 - level), 0).astype(jnp.float32) / (
        zero + bottom
    ).astype(jnp.float32)
    sigma = SIGMA_PEAK * upper * upper + SIGMA_PEAK * lower * lower
    for col, soil in enumerate(soils):
        rows = []
        for row in range(3):
            picked = jnp.zeros(shape, jnp.float32)
            for layer in range(layers):
                picked = jnp.where(soil == layer + 1.0, table[row, layer], picked)
            rows.append(picked)
        shear, lame, kappa = rows
        stiff = lame + shear
        diag_r = 6.0 * shear + 2.0 * stiff + kappa
        diag_i = kappa * sigma
        inside = soil > 0.0
        size = jnp.where(inside, diag_r * diag_r + diag_i * diag_i, 1.0)
        scale = jnp.where(inside, RELAX_WEIGHT / size, 0.0)
        both, quarter = shear + stiff, 0.25 * stiff
        values = {
            WR: scale * diag_r,
            WI: -scale * diag_i,
            A: shear,
            AB: both,
            H: quarter,
            AM: rolled_zero(shear, 1),
            ABM: rolled_zero(both, 1),
            HM: rolled_zero(quarter, 1),
            AP: rolled_zero(shear, -1),
            ABP: rolled_zero(both, -1),
            HP: rolled_zero(quarter, -1),
        }
        for j, value in values.items():
            coeffs[pl.ds((col * COEFFS + j) * depth, depth), :] = value


def tile_of(col):
    return (0, col) if col < HALO else (1, col - HALO) if col < HALO + WIDTH else (2, col - HALO - WIDTH)


def slot(z, col, pc):
    return (z * COLS + col) * PC + pc


def bottom_kernel(shots, depth, layers, own, left, right, table, widths, start, bottom, coeffs, v1, v2):
    tiles = (left, own, right)
    at = DEEP * WIDTH * PC * shots
    soils = []
    for col in range(COLS):
        which, place = tile_of(col)
        soils.append(tiles[which][pl.ds(at + place * depth, depth), :])
    fill_coeffs(coeffs, soils, table, widths, depth, layers)
    base = depth - DEEP

    def block(ref, number):
        return ref.at[pl.ds(number * shots, shots), :]

    for z in range(DEEP):
        for col in range(COLS):
            which, place = tile_of(col)
            coef = coef_of(coeffs, col, depth, base + z)
            for c in range(COMPS):
                fr = block(tiles[which], (z * WIDTH + place) * PC + c)[...]
                fi = block(tiles[which], (z * WIDTH + place) * PC + COMPS + c)[...]
                vr, vi = scaled(fr, fi, coef)
                block(v1, slot(z, col, c))[...] = vr
                block(v1, slot(z, col, COMPS + c))[...] = vi

    def first(x, z, pc):
        return block(v1, slot(z, x, pc))[...] if z < DEEP else None

    def second(x, z, pc):
        return block(v2, slot(z, x, pc))[...] if z < DEEP else None

    for z in range(1, DEEP):
        for x in range(1, COLS - 1):
            got = relaxed(memo(first), first, coef_of(coeffs, x, depth, base + z), x, z)
            for pc in range(PC):
                block(v2, slot(z, x, pc))[...] = got[pc]
    lane = lax.broadcasted_iota(jnp.int32, (shots, 2 * PATCH), 1)
    for x in range(HALO, HALO + WIDTH):
        got = relaxed(memo(second), first, coef_of(coeffs, x, depth, depth - 1), x, DEEP - 1)
        for pair in range(PC // 2):
            even, odd = got[2 * pair], got[2 * pair + 1]
            both = (
                jnp.where(lane < PATCH, even, pltpu.roll(odd, PATCH, 1)),
                jnp.where(lane < PATCH, pltpu.roll(even, PATCH, 1), odd),
            )
            for patch in range(2):
                where = (
                    pl.ds(((x - HALO) * 2 + patch) * shots, shots),
                    pl.ds(pair * 2 * PATCH, 2 * PATCH),
                )
                bottom[where] = both[patch] + start[where]


def full_kernel(shots, depth, coeffs, low, low_l, low_r, high, high_l, high_r, out, v1, v2):
    stride = PC * WIDTH * depth
    lows, highs = (low_l, low, low_r), (high_l, high, high_r)
    plane = COLS * PC * shots

    def at(z, col, pc):
        return pl.ds(pl.multiple_of((z + 1) * plane + (col * PC + pc) * shots, shots), shots)

    for ref in (v1, v2):
        for z in (-1, depth):
            for n in range(COLS * PC):
                ref[pl.ds((z + 1) * plane + n * shots, shots), :] = jnp.zeros((shots, 2 * PATCH), jnp.float32)

    def begin(tiles, shift):
        def run(z, carry):
            for col in range(COLS):
                which, place = tile_of(col)
                coef = coef_of(coeffs, col, depth, z)
                for c in range(COMPS):
                    number = ((z - shift) * WIDTH + place) * PC + c
                    fr = tiles[which][pl.ds(pl.multiple_of(number * shots, shots), shots), :]
                    fi = tiles[which][pl.ds(pl.multiple_of((number + COMPS) * shots, shots), shots), :]
                    vr, vi = scaled(fr, fi, coef)
                    v1[at(z, col, c), :] = vr
                    v1[at(z, col, COMPS + c), :] = vi
            return carry

        return run

    lax.fori_loop(0, depth - DEEP, begin(lows, 0), 0)
    lax.fori_loop(depth - DEEP, depth, begin(highs, depth - DEEP), 0)

    def first(x, z, pc):
        return v1[at(z, x, pc), :]

    def second(x, z, pc):
        return v2[at(z, x, pc), :]

    def middle(z, carry):
        for x in range(1, COLS - 1):
            got = relaxed(first, first, coef_of(coeffs, x, depth, z), x, z)
            for pc in range(PC):
                v2[at(z, x, pc), :] = got[pc]
        return carry

    lax.fori_loop(0, depth, middle, 0)

    def last(z, carry):
        for x in range(HALO, HALO + WIDTH):
            got = relaxed(second, first, coef_of(coeffs, x, depth, z), x, z)
            for pc in range(PC):
                out[pl.ds((pc * WIDTH + x - HALO) * depth + z, shots, stride=stride), :] = got[pc]
        return carry

    lax.fori_loop(0, depth, last, 0)


def inject_kernel(shots, depth, coeffs, own, l0, l1, r0, r1, base, out, v1, v2):
    stride = PC * WIDTH * depth

    def block(ref, number):
        return ref.at[pl.ds(number * shots, shots), :]

    lane = lax.broadcasted_iota(jnp.int32, (shots, 2 * PATCH), 1)
    for col in range(COLS):
        which, place = tile_of(col)
        coef = coef_of(coeffs, col, depth, 0)
        planes = []
        for pair in range(PC // 2):
            halves = []
            for patch in range(2):
                where = (
                    pl.ds((place * 2 + patch) * shots, shots),
                    pl.ds(pair * 2 * PATCH, 2 * PATCH),
                )
                halves.append((l0[where] + l1[where], own[where], r0[where] + r1[where])[which] if which != 1 else own[where])
            planes.append(jnp.where(lane < PATCH, halves[0], pltpu.roll(halves[1], PATCH, 1)))
            planes.append(jnp.where(lane < PATCH, pltpu.roll(halves[0], PATCH, 1), halves[1]))
        shear = coef(A)
        for c in range(COMPS):
            vr, vi = scaled(shear * planes[c], shear * planes[COMPS + c], coef)
            block(v1, slot(0, col, c))[...] = vr
            block(v1, slot(0, col, COMPS + c))[...] = vi

    def first(x, z, pc):
        return block(v1, slot(0, x, pc))[...] if z == 0 else None

    def second(x, z, pc):
        return block(v2, slot(z, x, pc))[...] if 0 <= z < 2 else None

    for z in range(2):
        for x in range(1, COLS - 1):
            got = relaxed(memo(first), first, coef_of(coeffs, x, depth, z), x, z)
            for pc in range(PC):
                block(v2, slot(z, x, pc))[...] = got[pc]
    out[...] = base[...]
    for z in range(3):
        for x in range(HALO, HALO + WIDTH):
            got = relaxed(memo(second), first, coef_of(coeffs, x, depth, z), x, z)
            for pc in range(PC):
                where = (pl.ds((pc * WIDTH + x - HALO) * depth + z, shots, stride=stride), slice(None))
                out[where] = base[where] + got[pc]


def split_kernel(blocks, high, low):
    whole = blocks[...]
    top = whole.astype(jnp.bfloat16)
    high[...] = top
    low[...] = (whole - top.astype(jnp.float32)).astype(jnp.bfloat16)


def product(shots, x, high, low, add, out):
    size = x.shape[1]
    for chain in range(x.shape[0] // shots):
        rows = pl.ds(chain * shots, shots)
        whole = x[rows, :]
        top = whole.astype(jnp.bfloat16)
        rest = (whole - top.astype(jnp.float32)).astype(jnp.bfloat16)
        block = pl.ds(chain * size, size)
        wide = jnp.dot(
            jnp.concatenate([top, rest], axis=0), high[block, :], preferred_element_type=jnp.float32
        )
        thin = jnp.dot(top, low[block, :], preferred_element_type=jnp.float32)
        total = wide[:shots] + wide[shots:] + thin
        out[rows, :] = total if add is None else total + add[rows, :]


def start_kernel(shots, slab, inflow, high, low, out):
    @pl.when(slab[0] == 0)
    def _():
        product(shots, inflow, high, low, None, out)

    @pl.when(slab[0] != 0)
    def _():
        out[...] = jnp.zeros(out.shape, jnp.float32)


def hop_kernel(shots, turn, slab, arrived, high, low, bottom, trace, held, new_trace, new_held):
    @pl.when(slab[0] == turn)
    def _():
        product(shots, arrived, high, low, bottom, new_trace)
        new_held[...] = arrived[...]

    @pl.when(slab[0] != turn)
    def _():
        new_trace[...] = trace[...]
        new_held[...] = held[...]


def per_device(source, soil_index, soil_table, pml_width, interface_blocks, inflow):
    shots, _, _, width, depth, length = source.shape
    layers = soil_table.shape[1]
    size = interface_blocks.shape[-1]
    slabs, tiles = lax.axis_size("slab"), lax.axis_size("tile")
    f32, bf16 = jnp.float32, jnp.bfloat16
    slab = lax.axis_index("slab").astype(jnp.int32).reshape(1)
    chains = width * (length // PATCH)
    low_rows = (depth - DEEP) * width * PC * shots
    high_rows = DEEP * width * PC * shots + width * depth

    def across(x, axes, moves):
        return lax.ppermute(x, axes, moves)

    up = [(t, t + 1) for t in range(tiles - 1)]
    down = [(t + 1, t) for t in range(tiles - 1)]

    def pairs(slab_moves, tile_moves):
        return [(a * tiles + t, b * tiles + u) for a, b in slab_moves for t, u in tile_moves]

    def both(x, moves):
        return lax.ppermute(x, ("slab", "tile"), moves)

    low, high = call(
        functools.partial(pack_kernel, shots, depth),
        [((low_rows, length), f32), ((high_rows, length), f32)],
        [source.reshape(-1, length), soil_index.reshape(-1, length)],
    )
    high_l = across(high, "tile", up)
    high_r = across(high, "tile", down)

    blocks = interface_blocks.reshape(chains * size, size)
    heavy, light = call(split_kernel, [(blocks.shape, bf16)] * 2, [blocks])
    held = inflow.reshape(chains * shots, size)
    row_shape = ((chains * shots, size), f32)
    (start,) = call(
        functools.partial(start_kernel, shots),
        [row_shape],
        [slab, held, heavy, light],
        [SMEM, VMEM, VMEM, VMEM],
    )
    bottom, coeffs = call(
        functools.partial(bottom_kernel, shots, depth, layers),
        [row_shape, ((COLS * COEFFS * depth, length), f32)],
        [high, high_l, high_r, soil_table, pml_width, start],
        [VMEM, VMEM, VMEM, SMEM, SMEM, VMEM],
        [pltpu.VMEM((DEEP * COLS * PC * shots, length), f32)] * 2,
    )

    trace = bottom
    halos = []
    low_l = low_r = solved = None
    for hop in range(slabs - 1):
        arrived = both(trace, pairs([(hop, hop + 1)], [(t, t) for t in range(tiles)]))
        if hop == slabs - 3:
            mine = jnp.where(slab[0] == hop, trace, held)
            moves = [(s, s) for s in range(hop)] + [(hop, hop + 1)]
            halos.append((both(mine, pairs(moves, up)), both(mine, pairs(moves, down))))
        if hop == slabs - 2:
            mine = jnp.where(slab[0] == hop, trace, held)
            moves = [(hop - 1, hop - 1), (hop, hop + 1)]
            halos.append((both(mine, pairs(moves, up)), both(mine, pairs(moves, down))))
        if hop == 1:
            ready, _ = lax.optimization_barrier((low, trace))
            low_l = across(ready, "tile", up)
            low_r = across(ready, "tile", down)
        if hop == slabs // 2:
            lows, _ = lax.optimization_barrier(((low, low_l, low_r), trace))
            (solved,) = call(
                functools.partial(full_kernel, shots, depth),
                [((shots * PC * width * depth, length), f32)],
                [coeffs, *lows, high, high_l, high_r],
                None,
                [pltpu.VMEM(((depth + 2) * COLS * PC * shots, length), f32)] * 2,
                flops=10_000_000,
            )
            arrived, solved = lax.optimization_barrier((arrived, solved))
        trace, held = call(
            functools.partial(hop_kernel, shots, hop + 1),
            [row_shape, row_shape],
            [slab, arrived, heavy, light, bottom, trace, held],
            [SMEM] + [VMEM] * 6,
        )
    (result,) = call(
        functools.partial(inject_kernel, shots, depth),
        [(solved.shape, f32)],
        [coeffs, held, halos[0][0], halos[1][0], halos[0][1], halos[1][1], solved],
        None,
        [pltpu.VMEM((DEEP * COLS * PC * shots, length), f32)] * 2,
    )
    traces = trace.reshape(width, 1, length // PATCH, shots, size)
    return result.reshape(source.shape), traces


def solution(mesh):
    in_specs = (
        P(None, None, None, "tile", "slab", None),
        P("tile", "slab", None),
        P(),
        P("slab", None),
        P("tile", "slab", None, None, None),
        P("tile", None, None, None),
    )
    out_specs = (P(None, None, None, "tile", "slab", None), P("tile", "slab", None, None, None))
    return jax.shard_map(
        per_device, mesh=mesh, in_specs=in_specs, out_specs=out_specs, check_vma=False
    )
```

```python
import functools

import jax
import jax.numpy as jnp
from jax import lax
from jax.experimental import pallas as pl
import jax.experimental.pallas.tpu as pltpu
from jax.sharding import PartitionSpec as P

PATCH = 64
RELAX_WEIGHT = 0.8
SIGMA_PEAK = 3.0
PARTS, COMPS = 2, 3
PC = PARTS * COMPS
WIDTH = 2
HALO = 2
COLS = WIDTH + 2 * HALO
DEEP = 3
COEFFS = 11
WR, WI, A, AB, H, AM, ABM, HM, AP, ABP, HP = range(COEFFS)
VMEM = pl.BlockSpec(memory_space=pltpu.VMEM)
SMEM = pl.BlockSpec(memory_space=pltpu.SMEM)
ANY = pl.BlockSpec(memory_space=pl.ANY)
MIB = 1024 * 1024
LIMIT = 6 * MIB
HOP_COST = 2_000_000_000
FULL_COST = 5_000_000_000


def call(name, body, outs, operands, specs=None, scratch=(), flops=0, limit=LIMIT):
    return pl.pallas_call(
        body,
        name=name,
        out_shape=[jax.ShapeDtypeStruct(shape, dtype) for shape, dtype in outs],
        in_specs=specs or [VMEM] * len(operands),
        out_specs=[VMEM] * len(outs),
        scratch_shapes=list(scratch),
        compiler_params=pltpu.CompilerParams(vmem_limit_bytes=limit),
        cost_estimate=pl.CostEstimate(flops=flops, bytes_accessed=1 << 20, transcendentals=0),
    )(*operands)


def put(src, target, shots, depth, d, col, pc, place):
    stride = PC * WIDTH * depth
    rows = src[pl.ds((pc * WIDTH + col) * depth + d, shots, stride=stride), :]
    target[pl.ds(((place * WIDTH + col) * PC + pc) * shots, shots), :] = rows


def pack_high_kernel(shots, depth, src_hbm, soil_hbm, high, src, soil, sems):
    copies = (
        pltpu.make_async_copy(src_hbm, src, sems.at[0]),
        pltpu.make_async_copy(soil_hbm, soil, sems.at[1]),
    )
    for copy in copies:
        copy.start()
    for copy in copies:
        copy.wait()
    for place in range(DEEP):
        for col in range(WIDTH):
            for pc in range(PC):
                put(src, high, shots, depth, depth - DEEP + place, col, pc, place)
    tail = pl.ds(DEEP * WIDTH * PC * shots, WIDTH * depth)
    high[tail, :] = (soil[...] + 1).astype(jnp.float32)


def pack_low_kernel(shots, depth, src, low):
    for d in range(depth - DEEP):
        for col in range(WIDTH):
            for pc in range(PC):
                put(src, low, shots, depth, d, col, pc, d)


def plus(*terms):
    terms = [t for t in terms if t is not None]
    return functools.reduce(lambda a, b: a + b, terms) if terms else None


def minus(a, b):
    if b is None:
        return a
    return -b if a is None else a - b


def times(c, a):
    return None if a is None else c * a


def coupling(field, coef, x, z):
    def step(c):
        return minus(field(x + 1, z, c), field(x - 1, z, c))

    def dive(col, c):
        return minus(field(col, z + 1, c), field(col, z - 1, c))

    def sides(c):
        return plus(field(x + 1, z, c), field(x - 1, z, c))

    def ends(c):
        return plus(field(x, z + 1, c), field(x, z - 1, c))

    length = 128
    results = []
    for c in range(COMPS):
        own = field(x, z, c)
        if c == 0:
            total = plus(
                times(coef(AB), sides(0)),
                times(coef(A), ends(0)),
                times(coef(H), minus(dive(x + 1, 2), dive(x - 1, 2))),
            )
            cross = step(1)
        elif c == 1:
            total = times(coef(A), plus(sides(1), ends(1)))
            cross = plus(step(0), dive(x, 2))
        else:
            total = plus(
                times(coef(A), sides(2)),
                times(coef(AB), ends(2)),
                times(coef(H), minus(dive(x + 1, 0), dive(x - 1, 0))),
            )
            cross = dive(x, 1)
        before, after = (ABM, ABP) if c == 1 else (AM, AP)
        ahead = plus(times(coef(before), own), times(coef(HM), cross))
        behind = minus(times(coef(after), own), times(coef(HP), cross))
        if ahead is not None:
            total = plus(total, pltpu.roll(ahead, length - 1, 1), pltpu.roll(behind, 1, 1))
        results.append(total)
    return results


def relaxed(field, first, coef, x, z):
    real = coupling(lambda i, k, c: field(i, k, c), coef, x, z)
    imag = coupling(lambda i, k, c: field(i, k, COMPS + c), coef, x, z)
    wr, wi = coef(WR), coef(WI)
    out = []
    for part in range(PARTS):
        for c in range(COMPS):
            pc = part * COMPS + c
            if part == 0:
                update = minus(times(wr, real[c]), times(wi, imag[c]))
            else:
                update = plus(times(wr, imag[c]), times(wi, real[c]))
            out.append(plus(times(1.0 - RELAX_WEIGHT, field(x, z, pc)), first(x, z, pc), update))
    return out


def scaled(fr, fi, coef):
    wr, wi = coef(WR), coef(WI)
    return wr * fr - wi * fi, wr * fi + wi * fr


def memo(fn):
    cache = {}

    def get(*key):
        if key not in cache:
            cache[key] = fn(*key)
        return cache[key]

    return get


def coef_of(coeffs, col, depth, z):
    return memo(lambda j: coeffs[pl.ds((col * COEFFS + j) * depth + z, 1), :])


def rolled_zero(x, shift):
    lane = lax.broadcasted_iota(jnp.int32, x.shape, 1)
    length = x.shape[1]
    if shift == 1:
        return jnp.where(lane == 0, 0.0, pltpu.roll(x, 1, 1))
    return jnp.where(lane == length - 1, 0.0, pltpu.roll(x, length - 1, 1))


def fill_coeffs(coeffs, soils, table, widths, depth, layers):
    shape = soils[0].shape
    level = lax.broadcasted_iota(jnp.int32, shape, 0)
    top, bottom = widths[0, 0], widths[0, 1]
    zero = jnp.zeros(shape, jnp.int32)
    upper = jnp.maximum(top - level, 0).astype(jnp.float32) / (zero + top).astype(jnp.float32)
    lower = jnp.maximum(bottom - (depth - 1 - level), 0).astype(jnp.float32) / (
        zero + bottom
    ).astype(jnp.float32)
    sigma = SIGMA_PEAK * upper * upper + SIGMA_PEAK * lower * lower
    for col, soil in enumerate(soils):
        rows = []
        for row in range(3):
            picked = jnp.zeros(shape, jnp.float32)
            for layer in range(layers):
                picked = jnp.where(soil == layer + 1.0, table[row, layer], picked)
            rows.append(picked)
        shear, lame, kappa = rows
        stiff = lame + shear
        diag_r = 6.0 * shear + 2.0 * stiff + kappa
        diag_i = kappa * sigma
        inside = soil > 0.0
        size = jnp.where(inside, diag_r * diag_r + diag_i * diag_i, 1.0)
        scale = jnp.where(inside, RELAX_WEIGHT / size, 0.0)
        both, quarter = shear + stiff, 0.25 * stiff
        values = {
            WR: scale * diag_r,
            WI: -scale * diag_i,
            A: shear,
            AB: both,
            H: quarter,
            AM: rolled_zero(shear, 1),
            ABM: rolled_zero(both, 1),
            HM: rolled_zero(quarter, 1),
            AP: rolled_zero(shear, -1),
            ABP: rolled_zero(both, -1),
            HP: rolled_zero(quarter, -1),
        }
        for j, value in values.items():
            coeffs[pl.ds((col * COEFFS + j) * depth, depth), :] = value


def tile_of(col):
    if col < HALO:
        return 0, col
    if col < HALO + WIDTH:
        return 1, col - HALO
    return 2, col - HALO - WIDTH


def slot(z, col, pc):
    return (z * COLS + col) * PC + pc


def bottom_kernel(shots, depth, layers, own, left, right, table, widths, start, bottom, coeffs, v1, v2):
    tiles = (left, own, right)
    at = DEEP * WIDTH * PC * shots
    soils = []
    for col in range(COLS):
        which, place = tile_of(col)
        soils.append(tiles[which][pl.ds(at + place * depth, depth), :])
    fill_coeffs(coeffs, soils, table, widths, depth, layers)
    base = depth - DEEP

    def block(ref, number):
        return ref.at[pl.ds(number * shots, shots), :]

    for z in range(DEEP):
        for col in range(COLS):
            which, place = tile_of(col)
            coef = coef_of(coeffs, col, depth, base + z)
            for c in range(COMPS):
                fr = block(tiles[which], (z * WIDTH + place) * PC + c)[...]
                fi = block(tiles[which], (z * WIDTH + place) * PC + COMPS + c)[...]
                vr, vi = scaled(fr, fi, coef)
                block(v1, slot(z, col, c))[...] = vr
                block(v1, slot(z, col, COMPS + c))[...] = vi

    def first(x, z, pc):
        return block(v1, slot(z, x, pc))[...] if z < DEEP else None

    def second(x, z, pc):
        return block(v2, slot(z, x, pc))[...] if z < DEEP else None

    for z in range(1, DEEP):
        for x in range(1, COLS - 1):
            got = relaxed(memo(first), first, coef_of(coeffs, x, depth, base + z), x, z)
            for pc in range(PC):
                block(v2, slot(z, x, pc))[...] = got[pc]
    lane = lax.broadcasted_iota(jnp.int32, (shots, 2 * PATCH), 1)
    for x in range(HALO, HALO + WIDTH):
        got = relaxed(memo(second), first, coef_of(coeffs, x, depth, depth - 1), x, DEEP - 1)
        for pair in range(PC // 2):
            even, odd = got[2 * pair], got[2 * pair + 1]
            both = (
                jnp.where(lane < PATCH, even, pltpu.roll(odd, PATCH, 1)),
                jnp.where(lane < PATCH, pltpu.roll(even, PATCH, 1), odd),
            )
            for patch in range(2):
                where = (
                    pl.ds(((x - HALO) * 2 + patch) * shots, shots),
                    pl.ds(pair * 2 * PATCH, 2 * PATCH),
                )
                bottom[where] = both[patch] + start[where]


def full_kernel(shots, depth, coeffs, low, low_l, low_r, high, high_l, high_r, out, v1, v2):
    stride = PC * WIDTH * depth
    lows, highs = (low_l, low, low_r), (high_l, high, high_r)
    plane = COLS * PC * shots

    def at(z, col, pc):
        return pl.ds(pl.multiple_of((z + 1) * plane + (col * PC + pc) * shots, shots), shots)

    for ref in (v1, v2):
        for z in (-1, depth):
            for n in range(COLS * PC):
                ref[pl.ds((z + 1) * plane + n * shots, shots), :] = jnp.zeros((shots, 2 * PATCH), jnp.float32)

    def begin(tiles, shift):
        def run(z, carry):
            for col in range(COLS):
                which, place = tile_of(col)
                coef = coef_of(coeffs, col, depth, z)
                for c in range(COMPS):
                    number = ((z - shift) * WIDTH + place) * PC + c
                    fr = tiles[which][pl.ds(pl.multiple_of(number * shots, shots), shots), :]
                    fi = tiles[which][pl.ds(pl.multiple_of((number + COMPS) * shots, shots), shots), :]
                    vr, vi = scaled(fr, fi, coef)
                    v1[at(z, col, c), :] = vr
                    v1[at(z, col, COMPS + c), :] = vi
            return carry

        return run

    lax.fori_loop(0, depth - DEEP, begin(lows, 0), 0)
    lax.fori_loop(depth - DEEP, depth, begin(highs, depth - DEEP), 0)

    def first(x, z, pc):
        return v1[at(z, x, pc), :]

    def second(x, z, pc):
        return v2[at(z, x, pc), :]

    def middle(z, carry):
        for x in range(1, COLS - 1):
            got = relaxed(first, first, coef_of(coeffs, x, depth, z), x, z)
            for pc in range(PC):
                v2[at(z, x, pc), :] = got[pc]
        return carry

    lax.fori_loop(0, depth, middle, 0)

    def last(z, carry):
        for x in range(HALO, HALO + WIDTH):
            got = relaxed(second, first, coef_of(coeffs, x, depth, z), x, z)
            for pc in range(PC):
                out[pl.ds((pc * WIDTH + x - HALO) * depth + z, shots, stride=stride), :] = got[pc]
        return carry

    lax.fori_loop(0, depth, last, 0)


def inject_kernel(shots, depth, coeffs, own, base, *refs):
    *halos, out, v1, v2 = refs
    half = len(halos) // 2
    sources = (halos[:half], [own], halos[half:])
    stride = PC * WIDTH * depth

    def block(ref, number):
        return ref.at[pl.ds(number * shots, shots), :]

    lane = lax.broadcasted_iota(jnp.int32, (shots, 2 * PATCH), 1)
    for col in range(COLS):
        which, place = tile_of(col)
        coef = coef_of(coeffs, col, depth, 0)
        planes = []
        for pair in range(PC // 2):
            halves = []
            for patch in range(2):
                where = (
                    pl.ds((place * 2 + patch) * shots, shots),
                    pl.ds(pair * 2 * PATCH, 2 * PATCH),
                )
                halves.append(plus(*[ref[where] for ref in sources[which]]))
            planes.append(jnp.where(lane < PATCH, halves[0], pltpu.roll(halves[1], PATCH, 1)))
            planes.append(jnp.where(lane < PATCH, pltpu.roll(halves[0], PATCH, 1), halves[1]))
        shear = coef(A)
        for c in range(COMPS):
            vr, vi = scaled(shear * planes[c], shear * planes[COMPS + c], coef)
            block(v1, slot(0, col, c))[...] = vr
            block(v1, slot(0, col, COMPS + c))[...] = vi

    def first(x, z, pc):
        return block(v1, slot(0, x, pc))[...] if z == 0 else None

    def second(x, z, pc):
        return block(v2, slot(z, x, pc))[...] if 0 <= z < 2 else None

    for z in range(2):
        for x in range(1, COLS - 1):
            got = relaxed(memo(first), first, coef_of(coeffs, x, depth, z), x, z)
            for pc in range(PC):
                block(v2, slot(z, x, pc))[...] = got[pc]
    out[...] = base[...]
    for z in range(3):
        for x in range(HALO, HALO + WIDTH):
            got = relaxed(memo(second), first, coef_of(coeffs, x, depth, z), x, z)
            for pc in range(PC):
                where = (pl.ds((pc * WIDTH + x - HALO) * depth + z, shots, stride=stride), slice(None))
                out[where] = base[where] + got[pc]


def split_kernel(blocks, high, low):
    whole = blocks[...]
    top = whole.astype(jnp.bfloat16)
    high[...] = top
    low[...] = (whole - top.astype(jnp.float32)).astype(jnp.bfloat16)


def product(shots, x, high, low, add, out):
    size = x.shape[1]
    for chain in range(x.shape[0] // shots):
        rows = pl.ds(chain * shots, shots)
        whole = x[rows, :]
        top = whole.astype(jnp.bfloat16)
        rest = (whole - top.astype(jnp.float32)).astype(jnp.bfloat16)
        block = pl.ds(chain * size, size)
        wide = jnp.dot(
            jnp.concatenate([top, rest], axis=0), high[block, :], preferred_element_type=jnp.float32
        )
        thin = jnp.dot(top, low[block, :], preferred_element_type=jnp.float32)
        total = wide[:shots] + wide[shots:] + thin
        out[rows, :] = total if add is None else total + add[rows, :]


def start_kernel(shots, inflow, high, low, out):
    slab = lax.axis_index("slab")

    @pl.when(slab == 0)
    def _():
        product(shots, inflow, high, low, None, out)

    @pl.when(slab != 0)
    def _():
        out[...] = jnp.zeros(out.shape, jnp.float32)


def hop_kernel(shots, turn, mixed, arrived, high, low, bottom, trace, held, *refs):
    slab = lax.axis_index("slab")
    half = max(len(refs) - 4, 0) // 2
    sides, (new_trace, new_held, *others) = refs[: 2 * half], refs[2 * half :]

    @pl.when(slab == turn)
    def _():
        product(shots, arrived, high, low, bottom, new_trace)
        new_held[...] = arrived[...]

    @pl.when(slab != turn)
    def _():
        new_trace[...] = trace[...]
        new_held[...] = held[...]

    if mixed:
        (mine,) = others

        @pl.when(slab == turn)
        def _():
            mine[...] = new_trace[...]

        @pl.when(slab != turn)
        def _():
            mine[...] = held[...]

    else:
        for number, ref in enumerate(others):
            ref[...] = plus(*[side[...] for side in sides[number * half : (number + 1) * half]])


def per_device(source, soil_index, soil_table, pml_width, interface_blocks, inflow):
    shots, _, _, width, depth, length = source.shape
    layers = soil_table.shape[1]
    size = interface_blocks.shape[-1]
    slabs, tiles = lax.axis_size("slab"), lax.axis_size("tile")
    f32, bf16 = jnp.float32, jnp.bfloat16
    chains = width * (length // PATCH)
    low_rows = (depth - DEEP) * width * PC * shots
    high_rows = DEEP * width * PC * shots + width * depth

    def across(x, axes, moves):
        return lax.ppermute(x, axes, moves)

    up = [(t, t + 1) for t in range(tiles - 1)]
    down = [(t + 1, t) for t in range(tiles - 1)]

    def pairs(slab_moves, tile_moves):
        return [(a * tiles + t, b * tiles + u) for a, b in slab_moves for t, u in tile_moves]

    def both(x, moves):
        return lax.ppermute(x, ("slab", "tile"), moves)

    src, soil = source.reshape(-1, length), soil_index.reshape(-1, length)
    (high,) = call(
        "pack_high",
        functools.partial(pack_high_kernel, shots, depth),
        [((high_rows, length), f32)],
        [pltpu.with_memory_space_constraint(x, pltpu.HBM) for x in (src, soil)],
        [ANY, ANY],
        [
            pltpu.VMEM(src.shape, f32),
            pltpu.VMEM(soil.shape, jnp.int32),
            pltpu.SemaphoreType.DMA((2,)),
        ],
    )
    high_l = across(high, "tile", up)
    high_r = across(high, "tile", down)

    blocks = interface_blocks.reshape(chains * size, size)
    heavy, light = call("split", split_kernel, [(blocks.shape, bf16)] * 2, [blocks])
    held = inflow.reshape(chains * shots, size)
    row_shape = ((chains * shots, size), f32)
    (start,) = call(
        "start",
        functools.partial(start_kernel, shots),
        [row_shape],
        [held, heavy, light],
    )
    bottom, coeffs = call(
        "bottom",
        functools.partial(bottom_kernel, shots, depth, layers),
        [row_shape, ((COLS * COEFFS * depth, length), f32)],
        [high, high_l, high_r, soil_table, pml_width, start],
        [VMEM, VMEM, VMEM, SMEM, SMEM, VMEM],
        [pltpu.VMEM((DEEP * COLS * PC * shots, length), f32)] * 2,
    )

    trace = bottom
    lefts, rights = [], []
    first_far = slabs // 2
    for hop in range(slabs - 1):
        arrived = both(trace, pairs([(hop, hop + 1)], [(t, t) for t in range(tiles)]))
        sides, mixed = [*lefts, *rights], first_far - 1 <= hop <= first_far
        if hop >= first_far:
            mine = gathered[0] if hop <= first_far + 1 else trace
            near = range(hop) if hop == first_far else [first_far] if hop == first_far + 1 else []
            moves = [(hop, hop + 1)] + [(s, s) for s in near]
            from_left, from_right = both(mine, pairs(moves, up)), both(mine, pairs(moves, down))
        if hop == 1:
            again, _ = lax.optimization_barrier((src, trace))
            (low,) = call(
                "pack_low",
                functools.partial(pack_low_kernel, shots, depth),
                [((low_rows, length), f32)],
                [again],
            )
            low_l = across(low, "tile", up)
            low_r = across(low, "tile", down)
        if hop == first_far - 1:
            lows, _ = lax.optimization_barrier(((low, low_l, low_r), trace))
            (solved,) = call(
                "full",
                functools.partial(full_kernel, shots, depth),
                [((shots * PC * width * depth, length), f32)],
                [coeffs, *lows, high, high_l, high_r],
                None,
                [pltpu.VMEM(((depth + 2) * COLS * PC * shots, length), f32)] * 2,
                flops=FULL_COST,
                limit=12 * MIB,
            )
            arrived, solved = lax.optimization_barrier((arrived, solved))
        trace, held, *gathered = call(
            f"hop{hop}",
            functools.partial(hop_kernel, shots, hop + 1, mixed),
            [row_shape] * (4 if sides else 3 if mixed else 2),
            [arrived, heavy, light, bottom, trace, held, *sides],
            flops=HOP_COST,
        )
        if hop >= first_far:
            done_l, done_r = ([], []) if mixed else (gathered[:1], gathered[1:])
            lefts, rights = done_l + [from_left], done_r + [from_right]
    (result,) = call(
        "inject",
        functools.partial(inject_kernel, shots, depth),
        [(solved.shape, f32)],
        [coeffs, held, solved, *lefts, *rights],
        None,
        [pltpu.VMEM((DEEP * COLS * PC * shots, length), f32)] * 2,
    )
    traces = trace.reshape(width, 1, length // PATCH, shots, size)
    return result.reshape(source.shape), traces


def solution(mesh):
    in_specs = (
        P(None, None, None, "tile", "slab", None),
        P("tile", "slab", None),
        P(),
        P("slab", None),
        P("tile", "slab", None, None, None),
        P("tile", None, None, None),
    )
    out_specs = (P(None, None, None, "tile", "slab", None), P("tile", "slab", None, None, None))
    return jax.shard_map(
        per_device, mesh=mesh, in_specs=in_specs, out_specs=out_specs, check_vma=False
    )
```

```python
import functools

import jax
import jax.numpy as jnp
from jax import lax
from jax.experimental import pallas as pl
import jax.experimental.pallas.tpu as pltpu
from jax.sharding import PartitionSpec as P

PATCH = 64
RELAX_WEIGHT = 0.8
SIGMA_PEAK = 3.0
PARTS, COMPS = 2, 3
PC = PARTS * COMPS
WIDTH = 2
HALO = 2
COLS = WIDTH + 2 * HALO
DEEP = 3
COEFFS = 11
WR, WI, A, AB, H, AM, ABM, HM, AP, ABP, HP = range(COEFFS)
VMEM = pl.BlockSpec(memory_space=pltpu.VMEM)
SMEM = pl.BlockSpec(memory_space=pltpu.SMEM)
ANY = pl.BlockSpec(memory_space=pl.ANY)
MIB = 1024 * 1024
LIMIT = 6 * MIB
HOP_COST = 2_000_000_000
LOW_COST = 2000000000.0
HOP_COSTS = (2000000000.0, 2000000000.0, 2000000000.0, 2000000000.0, 1000000.0, 1000000.0, 2000000000.0)
GATHER_COST = 2000000000.0
FULL_COST = 5_000_000_000


def call(name, body, outs, operands, specs=None, scratch=(), flops=5e8, limit=LIMIT):
    return pl.pallas_call(
        body,
        name=name,
        out_shape=[jax.ShapeDtypeStruct(shape, dtype) for shape, dtype in outs],
        in_specs=specs or [VMEM] * len(operands),
        out_specs=[VMEM] * len(outs),
        scratch_shapes=list(scratch),
        compiler_params=pltpu.CompilerParams(vmem_limit_bytes=limit),
        cost_estimate=pl.CostEstimate(flops=int(flops), bytes_accessed=0, transcendentals=0),
    )(*operands)


def put(src, target, shots, depth, d, col, pc, place):
    stride = PC * WIDTH * depth
    rows = src[pl.ds((pc * WIDTH + col) * depth + d, shots, stride=stride), :]
    target[pl.ds(((place * WIDTH + col) * PC + pc) * shots, shots), :] = rows


def pack_high_kernel(shots, depth, src_hbm, soil_hbm, high, src, soil, sems):
    copies = (
        pltpu.make_async_copy(src_hbm, src, sems.at[0]),
        pltpu.make_async_copy(soil_hbm, soil, sems.at[1]),
    )
    for copy in copies:
        copy.start()
    for copy in copies:
        copy.wait()
    for place in range(DEEP):
        for col in range(WIDTH):
            for pc in range(PC):
                put(src, high, shots, depth, depth - DEEP + place, col, pc, place)
    tail = pl.ds(DEEP * WIDTH * PC * shots, WIDTH * depth)
    high[tail, :] = (soil[...] + 1).astype(jnp.float32)


def pack_low_kernel(shots, depth, src, low):
    for d in range(depth - DEEP):
        for col in range(WIDTH):
            for pc in range(PC):
                put(src, low, shots, depth, d, col, pc, d)


def plus(*terms):
    terms = [t for t in terms if t is not None]
    return functools.reduce(lambda a, b: a + b, terms) if terms else None


def minus(a, b):
    if b is None:
        return a
    return -b if a is None else a - b


def times(c, a):
    return None if a is None else c * a


def coupling(field, coef, x, z):
    def step(c):
        return minus(field(x + 1, z, c), field(x - 1, z, c))

    def dive(col, c):
        return minus(field(col, z + 1, c), field(col, z - 1, c))

    def sides(c):
        return plus(field(x + 1, z, c), field(x - 1, z, c))

    def ends(c):
        return plus(field(x, z + 1, c), field(x, z - 1, c))

    length = 128
    results = []
    for c in range(COMPS):
        own = field(x, z, c)
        if c == 0:
            total = plus(
                times(coef(AB), sides(0)),
                times(coef(A), ends(0)),
                times(coef(H), minus(dive(x + 1, 2), dive(x - 1, 2))),
            )
            cross = step(1)
        elif c == 1:
            total = times(coef(A), plus(sides(1), ends(1)))
            cross = plus(step(0), dive(x, 2))
        else:
            total = plus(
                times(coef(A), sides(2)),
                times(coef(AB), ends(2)),
                times(coef(H), minus(dive(x + 1, 0), dive(x - 1, 0))),
            )
            cross = dive(x, 1)
        before, after = (ABM, ABP) if c == 1 else (AM, AP)
        ahead = plus(times(coef(before), own), times(coef(HM), cross))
        behind = minus(times(coef(after), own), times(coef(HP), cross))
        if ahead is not None:
            total = plus(total, pltpu.roll(ahead, length - 1, 1), pltpu.roll(behind, 1, 1))
        results.append(total)
    return results


def relaxed(field, first, coef, x, z):
    real = coupling(lambda i, k, c: field(i, k, c), coef, x, z)
    imag = coupling(lambda i, k, c: field(i, k, COMPS + c), coef, x, z)
    wr, wi = coef(WR), coef(WI)
    out = []
    for part in range(PARTS):
        for c in range(COMPS):
            pc = part * COMPS + c
            if part == 0:
                update = minus(times(wr, real[c]), times(wi, imag[c]))
            else:
                update = plus(times(wr, imag[c]), times(wi, real[c]))
            out.append(plus(times(1.0 - RELAX_WEIGHT, field(x, z, pc)), first(x, z, pc), update))
    return out


def scaled(fr, fi, coef):
    wr, wi = coef(WR), coef(WI)
    return wr * fr - wi * fi, wr * fi + wi * fr


def memo(fn):
    cache = {}

    def get(*key):
        if key not in cache:
            cache[key] = fn(*key)
        return cache[key]

    return get


def coef_of(coeffs, col, depth, z):
    return memo(lambda j: coeffs[pl.ds((col * COEFFS + j) * depth + z, 1), :])


def rolled_zero(x, shift):
    lane = lax.broadcasted_iota(jnp.int32, x.shape, 1)
    length = x.shape[1]
    if shift == 1:
        return jnp.where(lane == 0, 0.0, pltpu.roll(x, 1, 1))
    return jnp.where(lane == length - 1, 0.0, pltpu.roll(x, length - 1, 1))


def fill_coeffs(coeffs, soils, table, widths, depth, layers):
    shape = soils[0].shape
    level = lax.broadcasted_iota(jnp.int32, shape, 0)
    top, bottom = widths[0, 0], widths[0, 1]
    zero = jnp.zeros(shape, jnp.int32)
    upper = jnp.maximum(top - level, 0).astype(jnp.float32) / (zero + top).astype(jnp.float32)
    lower = jnp.maximum(bottom - (depth - 1 - level), 0).astype(jnp.float32) / (
        zero + bottom
    ).astype(jnp.float32)
    sigma = SIGMA_PEAK * upper * upper + SIGMA_PEAK * lower * lower
    for col, soil in enumerate(soils):
        rows = []
        for row in range(3):
            picked = jnp.zeros(shape, jnp.float32)
            for layer in range(layers):
                picked = jnp.where(soil == layer + 1.0, table[row, layer], picked)
            rows.append(picked)
        shear, lame, kappa = rows
        stiff = lame + shear
        diag_r = 6.0 * shear + 2.0 * stiff + kappa
        diag_i = kappa * sigma
        inside = soil > 0.0
        size = jnp.where(inside, diag_r * diag_r + diag_i * diag_i, 1.0)
        scale = jnp.where(inside, RELAX_WEIGHT / size, 0.0)
        both, quarter = shear + stiff, 0.25 * stiff
        values = {
            WR: scale * diag_r,
            WI: -scale * diag_i,
            A: shear,
            AB: both,
            H: quarter,
            AM: rolled_zero(shear, 1),
            ABM: rolled_zero(both, 1),
            HM: rolled_zero(quarter, 1),
            AP: rolled_zero(shear, -1),
            ABP: rolled_zero(both, -1),
            HP: rolled_zero(quarter, -1),
        }
        for j, value in values.items():
            coeffs[pl.ds((col * COEFFS + j) * depth, depth), :] = value


def tile_of(col):
    if col < HALO:
        return 0, col
    if col < HALO + WIDTH:
        return 1, col - HALO
    return 2, col - HALO - WIDTH


def pick(which, own, off, on, read):
    if which == 1:
        return read(own)
    even = lax.axis_index("tile") % 2 == 0
    first, second = read(off), read(on)
    return jnp.where(even, first, second) if which == 0 else jnp.where(even, second, first)


def slot(z, col, pc):
    return (z * COLS + col) * PC + pc


def bottom_kernel(shots, depth, layers, first_only, own, off, on, table, widths, start, *refs):
    bottoms, coeffs, v1, v2 = refs[:WIDTH], *refs[WIDTH:]
    work = functools.partial(
        bottom_planes, shots, depth, layers, own, off, on, table, widths, start, bottoms, coeffs, v1, v2
    )
    if not first_only:
        work()
        return
    slab = lax.axis_index("slab")
    pl.when(slab == 0)(work)

    @pl.when(slab != 0)
    def _():
        for ref in bottoms:
            ref[...] = jnp.zeros(ref.shape, jnp.float32)


def bottom_planes(shots, depth, layers, own, off, on, table, widths, start, bottoms, coeffs, v1, v2):
    at = DEEP * WIDTH * PC * shots
    soils = []
    for col in range(COLS):
        which, place = tile_of(col)
        where = pl.ds(at + place * depth, depth)
        soils.append(pick(which, own, off, on, lambda ref: ref[where, :]))
    fill_coeffs(coeffs, soils, table, widths, depth, layers)
    base = depth - DEEP

    def block(ref, number):
        return ref.at[pl.ds(number * shots, shots), :]

    for z in range(DEEP):
        for col in range(COLS):
            which, place = tile_of(col)
            coef = coef_of(coeffs, col, depth, base + z)
            for c in range(COMPS):
                fr, fi = (
                    pick(which, own, off, on, lambda ref: block(ref, (z * WIDTH + place) * PC + pc)[...])
                    for pc in (c, COMPS + c)
                )
                vr, vi = scaled(fr, fi, coef)
                block(v1, slot(z, col, c))[...] = vr
                block(v1, slot(z, col, COMPS + c))[...] = vi

    def first(x, z, pc):
        return block(v1, slot(z, x, pc))[...] if z < DEEP else None

    def second(x, z, pc):
        return block(v2, slot(z, x, pc))[...] if z < DEEP else None

    for z in range(1, DEEP):
        for x in range(1, COLS - 1):
            got = relaxed(memo(first), first, coef_of(coeffs, x, depth, base + z), x, z)
            for pc in range(PC):
                block(v2, slot(z, x, pc))[...] = got[pc]
    lane = lax.broadcasted_iota(jnp.int32, (shots, 2 * PATCH), 1)
    for x in range(HALO, HALO + WIDTH):
        got = relaxed(memo(second), first, coef_of(coeffs, x, depth, depth - 1), x, DEEP - 1)
        for pair in range(PC // 2):
            even, odd = got[2 * pair], got[2 * pair + 1]
            both = (
                jnp.where(lane < PATCH, even, pltpu.roll(odd, PATCH, 1)),
                jnp.where(lane < PATCH, pltpu.roll(even, PATCH, 1), odd),
            )
            for patch in range(2):
                lanes = pl.ds(pair * 2 * PATCH, 2 * PATCH)
                given = start[pl.ds(((x - HALO) * 2 + patch) * shots, shots), lanes]
                bottoms[x - HALO][pl.ds(patch * shots, shots), lanes] = both[patch] + given


def full_kernel(shots, depth, coeffs, low, low_off, low_on, high, high_off, high_on, out, v1, v2):
    stride = PC * WIDTH * depth
    lows, highs = (low, low_off, low_on), (high, high_off, high_on)
    plane = COLS * PC * shots

    def at(z, col, pc):
        return pl.ds(pl.multiple_of((z + 1) * plane + (col * PC + pc) * shots, shots), shots)

    for ref in (v1, v2):
        for z in (-1, depth):
            for n in range(COLS * PC):
                ref[pl.ds((z + 1) * plane + n * shots, shots), :] = jnp.zeros((shots, 2 * PATCH), jnp.float32)

    def begin(tiles, shift):
        def run(z, carry):
            for col in range(COLS):
                which, place = tile_of(col)
                coef = coef_of(coeffs, col, depth, z)
                for c in range(COMPS):
                    number = ((z - shift) * WIDTH + place) * PC + c
                    fr, fi = (
                        pick(which, *tiles, lambda ref: ref[pl.ds(pl.multiple_of(n * shots, shots), shots), :])
                        for n in (number, number + COMPS)
                    )
                    vr, vi = scaled(fr, fi, coef)
                    v1[at(z, col, c), :] = vr
                    v1[at(z, col, COMPS + c), :] = vi
            return carry

        return run

    lax.fori_loop(0, depth - DEEP, begin(lows, 0), 0)
    lax.fori_loop(depth - DEEP, depth, begin(highs, depth - DEEP), 0)

    def first(x, z, pc):
        return v1[at(z, x, pc), :]

    def second(x, z, pc):
        return v2[at(z, x, pc), :]

    def middle(z, carry):
        for x in range(1, COLS - 1):
            got = relaxed(first, first, coef_of(coeffs, x, depth, z), x, z)
            for pc in range(PC):
                v2[at(z, x, pc), :] = got[pc]
        return carry

    lax.fori_loop(0, depth, middle, 0)

    def last(z, carry):
        for x in range(HALO, HALO + WIDTH):
            got = relaxed(second, first, coef_of(coeffs, x, depth, z), x, z)
            for pc in range(PC):
                out[pl.ds((pc * WIDTH + x - HALO) * depth + z, shots, stride=stride), :] = got[pc]
        return carry

    lax.fori_loop(0, depth, last, 0)


def inject_kernel(shots, depth, coeffs, base, *refs):
    own, halos, (out, v1, v2) = refs[:WIDTH], refs[WIDTH:-3], refs[-3:]
    half = len(halos) // 2
    off, on = halos[:half], halos[half:]
    stride = PC * WIDTH * depth

    def block(ref, number):
        return ref.at[pl.ds(number * shots, shots), :]

    lane = lax.broadcasted_iota(jnp.int32, (shots, 2 * PATCH), 1)
    for col in range(COLS):
        which, place = tile_of(col)
        coef = coef_of(coeffs, col, depth, 0)
        planes = []
        for pair in range(PC // 2):
            halves = []
            for patch in range(2):
                where = (
                    pl.ds((place * 2 + patch) * shots, shots),
                    pl.ds(pair * 2 * PATCH, 2 * PATCH),
                )
                if which == 1:
                    halves.append(own[place][pl.ds(patch * shots, shots), where[1]])
                else:
                    halves.append(
                        pick(which, None, off, on, lambda refs: plus(*[ref[where] for ref in refs]))
                    )
            planes.append(jnp.where(lane < PATCH, halves[0], pltpu.roll(halves[1], PATCH, 1)))
            planes.append(jnp.where(lane < PATCH, pltpu.roll(halves[0], PATCH, 1), halves[1]))
        shear = coef(A)
        for c in range(COMPS):
            vr, vi = scaled(shear * planes[c], shear * planes[COMPS + c], coef)
            block(v1, slot(0, col, c))[...] = vr
            block(v1, slot(0, col, COMPS + c))[...] = vi

    def first(x, z, pc):
        return block(v1, slot(0, x, pc))[...] if z == 0 else None

    def second(x, z, pc):
        return block(v2, slot(z, x, pc))[...] if 0 <= z < 2 else None

    for z in range(2):
        for x in range(1, COLS - 1):
            got = relaxed(memo(first), first, coef_of(coeffs, x, depth, z), x, z)
            for pc in range(PC):
                block(v2, slot(z, x, pc))[...] = got[pc]
    out[...] = base[...]
    for z in range(3):
        for x in range(HALO, HALO + WIDTH):
            got = relaxed(memo(second), first, coef_of(coeffs, x, depth, z), x, z)
            for pc in range(PC):
                where = (pl.ds((pc * WIDTH + x - HALO) * depth + z, shots, stride=stride), slice(None))
                out[where] = base[where] + got[pc]


def split_kernel(blocks, high, low):
    whole = blocks[...]
    top = whole.astype(jnp.bfloat16)
    high[...] = top
    low[...] = (whole - top.astype(jnp.float32)).astype(jnp.bfloat16)


def product(shots, x, high, low, add, out, first):
    size = x.shape[1]
    for chain in range(x.shape[0] // shots):
        rows = pl.ds(chain * shots, shots)
        whole = x[rows, :]
        top = whole.astype(jnp.bfloat16)
        rest = (whole - top.astype(jnp.float32)).astype(jnp.bfloat16)
        block = pl.ds((first + chain) * size, size)
        wide = jnp.dot(
            jnp.concatenate([top, rest], axis=0), high[block, :], preferred_element_type=jnp.float32
        )
        thin = jnp.dot(top, low[block, :], preferred_element_type=jnp.float32)
        total = wide[:shots] + wide[shots:] + thin
        out[rows, :] = total if add is None else total + add[rows, :]


def start_kernel(shots, inflow, high, low, out, *helds):
    slab = lax.axis_index("slab")

    @pl.when(slab == 0)
    def _():
        product(shots, inflow, high, low, None, out, 0)

    @pl.when(slab != 0)
    def _():
        out[...] = jnp.zeros(out.shape, jnp.float32)

    for col, ref in enumerate(helds):
        ref[...] = inflow[pl.ds(col * ref.shape[0], ref.shape[0]), :]


def hop_kernel(shots, turn, col, groups, *refs):
    arrived, high, low, bottom, trace, held, *rest = refs
    sides, (new_trace, new_held, *sums) = rest[: sum(groups)], rest[sum(groups) :]
    slab = lax.axis_index("slab")

    @pl.when(slab == turn)
    def _():
        product(shots, arrived, high, low, bottom, new_trace, col * (arrived.shape[0] // shots))
        new_held[...] = arrived[...]

    @pl.when(slab != turn)
    def _():
        new_trace[...] = trace[...]
        new_held[...] = held[...]

    for ref, count in zip(sums, [g for g in groups if g]):
        ref[...] = plus(*[side[...] for side in sides[:count]])
        sides = sides[count:]


def gather_kernel(turn, *refs):
    mine, rows = refs[-1], refs[0].shape[0]
    traces, helds = refs[:WIDTH], refs[WIDTH:-1]

    def fill(parts):
        for number, part in enumerate(parts):
            mine[pl.ds(number * rows, rows), :] = part[...]

    slab = lax.axis_index("slab")
    pl.when(slab == turn)(lambda: fill(traces))
    pl.when(slab != turn)(lambda: fill(helds))


def per_device(source, soil_index, soil_table, pml_width, interface_blocks, inflow):
    shots, _, _, width, depth, length = source.shape
    layers = soil_table.shape[1]
    size = interface_blocks.shape[-1]
    slabs, tiles = lax.axis_size("slab"), lax.axis_size("tile")
    f32, bf16 = jnp.float32, jnp.bfloat16
    chains = width * (length // PATCH)
    low_rows = (depth - DEEP) * width * PC * shots
    high_rows = DEEP * width * PC * shots + width * depth

    off = [p for t in range(1, tiles - 1, 2) for p in ((t, t + 1), (t + 1, t))]
    on = [p for t in range(0, tiles - 1, 2) for p in ((t, t + 1), (t + 1, t))]

    def exchange(x):
        return lax.ppermute(x, "tile", off), lax.ppermute(x, "tile", on)

    def pairs(slab_moves, tile_moves):
        return [(a * tiles + t, b * tiles + u) for a, b in slab_moves for t, u in tile_moves]

    def both(x, moves):
        return lax.ppermute(x, ("slab", "tile"), moves)

    src, soil = source.reshape(-1, length), soil_index.reshape(-1, length)
    (high,) = call(
        "pack_high",
        functools.partial(pack_high_kernel, shots, depth),
        [((high_rows, length), f32)],
        [pltpu.with_memory_space_constraint(x, pltpu.HBM) for x in (src, soil)],
        [ANY, ANY],
        [
            pltpu.VMEM(src.shape, f32),
            pltpu.VMEM(soil.shape, jnp.int32),
            pltpu.SemaphoreType.DMA((2,)),
        ],
    )
    high_off, high_on = exchange(high)

    blocks = interface_blocks.reshape(chains * size, size)
    heavy, light = call("split", split_kernel, [(blocks.shape, bf16)] * 2, [blocks])
    held = inflow.reshape(chains * shots, size)
    row_shape = ((chains * shots, size), f32)
    chunk = (chains // width * shots, size)
    start, *helds = call(
        "start",
        functools.partial(start_kernel, shots),
        [row_shape] + [(chunk, f32)] * width,
        [held, heavy, light],
    )
    table_shape = (COLS * COEFFS * depth, length)
    planes = [pltpu.VMEM((DEEP * COLS * PC * shots, length), f32)] * 2
    near = [high, high_off, high_on, soil_table, pml_width, start]
    near_specs = [VMEM, VMEM, VMEM, SMEM, SMEM, VMEM]
    traces = call(
        "first",
        functools.partial(bottom_kernel, shots, depth, layers, True),
        [(chunk, f32)] * width,
        near,
        near_specs,
        [pltpu.VMEM(table_shape, f32)] + planes,
    )
    *bottoms, coeffs = call(
        "bottom",
        functools.partial(bottom_kernel, shots, depth, layers, False),
        [(chunk, f32)] * width + [(table_shape, f32)],
        near,
        near_specs,
        planes,
        flops=HOP_COST,
    )
    offs, ons = [], []
    first_far, mine = slabs // 2, None
    for hop in range(slabs - 1):
        step = pairs([(hop, hop + 1)], [(t, t) for t in range(tiles)])
        arrived = [both(trace, step) for trace in traces]
        groups = (len(offs), len(ons))
        sides = [*offs, *ons]
        from_off, from_on = [], []
        if hop >= first_far:
            same = range(hop) if hop == first_far else [first_far] if hop == first_far + 1 else []
            from_off = [both(mine, pairs([(hop, hop + 1)] + [(s, s) for s in same], off))]
        if hop > first_far:
            same = range(hop) if hop == slabs - 2 else []
            from_on = [both(mine, pairs([(hop, hop + 1)] + [(s, s) for s in same], on))]
        if hop == 1:
            again, _ = lax.optimization_barrier((src, traces))
            (low,) = call(
                "pack_low",
                functools.partial(pack_low_kernel, shots, depth),
                [((low_rows, length), f32)],
                [again],
                flops=LOW_COST,
            )
            low_off, low_on = exchange(low)
        if hop == first_far - 1:
            lows, _ = lax.optimization_barrier(((low, low_off, low_on), traces))
            (solved,) = call(
                "full",
                functools.partial(full_kernel, shots, depth),
                [((shots * PC * width * depth, length), f32)],
                [coeffs, *lows, high, high_off, high_on],
                None,
                [pltpu.VMEM(((depth + 2) * COLS * PC * shots, length), f32)] * 2,
                flops=FULL_COST,
                limit=12 * MIB,
            )
            arrived, solved = lax.optimization_barrier((arrived, solved))
        if hop in (1, slabs - 2):
            arrived = lax.optimization_barrier(arrived)
        new_traces, new_helds = [], []
        for col in range(width):
            counts = groups if col == width - 1 else (0, 0)
            trace, kept, *sums = call(
                f"hop{hop}_{col}",
                functools.partial(hop_kernel, shots, hop + 1, col, counts),
                [(chunk, f32)] * 2 + [row_shape] * sum(c > 0 for c in counts),
                [arrived[col], heavy, light, bottoms[col], traces[col], helds[col]]
                + (sides if col == width - 1 else []),
                flops=HOP_COSTS[hop],
            )
            new_traces.append(trace)
            new_helds.append(kept)
        traces, helds = new_traces, new_helds
        if first_far - 1 <= hop < slabs - 2:
            (mine,) = call(
                f"gather{hop}",
                functools.partial(gather_kernel, hop + 1),
                [row_shape],
                [*traces, *helds],
                flops=GATHER_COST,
            )
        offs = ([sums.pop(0)] if groups[0] else []) + from_off
        ons = ([sums.pop(0)] if groups[1] else []) + from_on
    (whole,) = call("whole", functools.partial(gather_kernel, slabs), [row_shape], [*helds, *traces])
    (result,) = call(
        "inject",
        functools.partial(inject_kernel, shots, depth),
        [(solved.shape, f32)],
        [coeffs, solved, *helds, *offs, *ons],
        None,
        planes,
    )
    traces = whole.reshape(width, 1, length // PATCH, shots, size)
    return result.reshape(source.shape), traces


def solution(mesh):
    in_specs = (
        P(None, None, None, "tile", "slab", None),
        P("tile", "slab", None),
        P(),
        P("slab", None),
        P("tile", "slab", None, None, None),
        P("tile", None, None, None),
    )
    out_specs = (P(None, None, None, "tile", "slab", None), P("tile", "slab", None, None, None))
    return jax.shard_map(
        per_device, mesh=mesh, in_specs=in_specs, out_specs=out_specs, check_vma=False
    )
```

```python
import functools

import jax
import jax.numpy as jnp
from jax import lax
from jax.experimental import pallas as pl
import jax.experimental.pallas.tpu as pltpu
from jax.sharding import PartitionSpec as P

PATCH = 64
RELAX_WEIGHT = 0.8
SIGMA_PEAK = 3.0
PARTS, COMPS = 2, 3
PC = PARTS * COMPS
WIDTH = 2
HALO = 2
COLS = WIDTH + 2 * HALO
DEEP = 3
COEFFS = 11
WR, WI, A, AB, H, AM, ABM, HM, AP, ABP, HP = range(COEFFS)
VMEM = pl.BlockSpec(memory_space=pltpu.VMEM)
SMEM = pl.BlockSpec(memory_space=pltpu.SMEM)
ANY = pl.BlockSpec(memory_space=pl.ANY)
MIB = 1024 * 1024
LIMIT = 6 * MIB
HOP_COST = 2e9
LOW_COST = 2e9
HOP_COSTS = (2e9, 2e9, 2e9, 2e9, 1e6, 1e6, 2e9)
GATHER_COST = 2e9
FULL_COST = 5e9


def call(name, body, outs, operands, specs=None, scratch=(), flops=5e8, limit=LIMIT):
    return pl.pallas_call(
        body,
        name=name,
        out_shape=[jax.ShapeDtypeStruct(shape, dtype) for shape, dtype in outs],
        in_specs=specs or [VMEM] * len(operands),
        out_specs=[VMEM] * len(outs),
        scratch_shapes=list(scratch),
        compiler_params=pltpu.CompilerParams(vmem_limit_bytes=limit),
        cost_estimate=pl.CostEstimate(flops=int(flops), bytes_accessed=0, transcendentals=0),
    )(*operands)


def put(src, target, shots, depth, d, col, pc, place):
    stride = PC * WIDTH * depth
    rows = src[pl.ds((pc * WIDTH + col) * depth + d, shots, stride=stride), :]
    target[pl.ds(((place * WIDTH + col) * PC + pc) * shots, shots), :] = rows


def pack_high_kernel(shots, depth, src_hbm, soil_hbm, high, src, soil, sems):
    copies = (
        pltpu.make_async_copy(src_hbm, src, sems.at[0]),
        pltpu.make_async_copy(soil_hbm, soil, sems.at[1]),
    )
    for copy in copies:
        copy.start()
    for copy in copies:
        copy.wait()
    for place in range(DEEP):
        for col in range(WIDTH):
            for pc in range(PC):
                put(src, high, shots, depth, depth - DEEP + place, col, pc, place)
    tail = pl.ds(DEEP * WIDTH * PC * shots, WIDTH * depth)
    high[tail, :] = (soil[...] + 1).astype(jnp.float32)


def pack_low_kernel(shots, depth, src, low):
    for d in range(depth - DEEP):
        for col in range(WIDTH):
            for pc in range(PC):
                put(src, low, shots, depth, d, col, pc, d)


def plus(*terms):
    terms = [t for t in terms if t is not None]
    return functools.reduce(lambda a, b: a + b, terms) if terms else None


def minus(a, b):
    if b is None:
        return a
    return -b if a is None else a - b


def times(c, a):
    return None if a is None else c * a


def coupling(field, coef, x, z):
    def step(c):
        return minus(field(x + 1, z, c), field(x - 1, z, c))

    def dive(col, c):
        return minus(field(col, z + 1, c), field(col, z - 1, c))

    def sides(c):
        return plus(field(x + 1, z, c), field(x - 1, z, c))

    def ends(c):
        return plus(field(x, z + 1, c), field(x, z - 1, c))

    length = 128
    results = []
    for c in range(COMPS):
        own = field(x, z, c)
        if c == 0:
            total = plus(
                times(coef(AB), sides(0)),
                times(coef(A), ends(0)),
                times(coef(H), minus(dive(x + 1, 2), dive(x - 1, 2))),
            )
            cross = step(1)
        elif c == 1:
            total = times(coef(A), plus(sides(1), ends(1)))
            cross = plus(step(0), dive(x, 2))
        else:
            total = plus(
                times(coef(A), sides(2)),
                times(coef(AB), ends(2)),
                times(coef(H), minus(dive(x + 1, 0), dive(x - 1, 0))),
            )
            cross = dive(x, 1)
        before, after = (ABM, ABP) if c == 1 else (AM, AP)
        ahead = plus(times(coef(before), own), times(coef(HM), cross))
        behind = minus(times(coef(after), own), times(coef(HP), cross))
        if ahead is not None:
            total = plus(total, pltpu.roll(ahead, length - 1, 1), pltpu.roll(behind, 1, 1))
        results.append(total)
    return results


def relaxed(field, first, coef, x, z):
    real = coupling(lambda i, k, c: field(i, k, c), coef, x, z)
    imag = coupling(lambda i, k, c: field(i, k, COMPS + c), coef, x, z)
    wr, wi = coef(WR), coef(WI)
    out = []
    for part in range(PARTS):
        for c in range(COMPS):
            pc = part * COMPS + c
            if part == 0:
                update = minus(times(wr, real[c]), times(wi, imag[c]))
            else:
                update = plus(times(wr, imag[c]), times(wi, real[c]))
            out.append(plus(times(1.0 - RELAX_WEIGHT, field(x, z, pc)), first(x, z, pc), update))
    return out


def scaled(fr, fi, coef):
    wr, wi = coef(WR), coef(WI)
    return wr * fr - wi * fi, wr * fi + wi * fr


def memo(fn):
    cache = {}

    def get(*key):
        if key not in cache:
            cache[key] = fn(*key)
        return cache[key]

    return get


def coef_of(coeffs, col, depth, z):
    return memo(lambda j: coeffs[pl.ds((col * COEFFS + j) * depth + z, 1), :])


def rolled_zero(x, shift):
    lane = lax.broadcasted_iota(jnp.int32, x.shape, 1)
    length = x.shape[1]
    if shift == 1:
        return jnp.where(lane == 0, 0.0, pltpu.roll(x, 1, 1))
    return jnp.where(lane == length - 1, 0.0, pltpu.roll(x, length - 1, 1))


def consts_kernel(depth, layers, table, widths, out):
    shape = (depth, out.shape[1])
    level = lax.broadcasted_iota(jnp.int32, shape, 0)
    top, bottom = widths[0, 0], widths[0, 1]
    zero = jnp.zeros(shape, jnp.int32)
    upper = jnp.maximum(top - level, 0).astype(jnp.float32) / (zero + top).astype(jnp.float32)
    lower = jnp.maximum(bottom - (depth - 1 - level), 0).astype(jnp.float32) / (
        zero + bottom
    ).astype(jnp.float32)
    out[pl.ds(0, depth), :] = SIGMA_PEAK * upper * upper + SIGMA_PEAK * lower * lower
    for row in range(3):
        for layer in range(layers):
            value = jnp.full((1, out.shape[1]), table[row, layer], jnp.float32)
            out[pl.ds(depth + row * layers + layer, 1), :] = value


def fill_coeffs(coeffs, soils, consts, depth, layers):
    shape = soils[0].shape
    sigma = consts[pl.ds(0, depth), :]
    for col, soil in enumerate(soils):
        rows = []
        for row in range(3):
            picked = jnp.zeros(shape, jnp.float32)
            for layer in range(layers):
                value = consts[pl.ds(depth + row * layers + layer, 1), :]
                picked = jnp.where(soil == layer + 1.0, value, picked)
            rows.append(picked)
        shear, lame, kappa = rows
        stiff = lame + shear
        diag_r = 6.0 * shear + 2.0 * stiff + kappa
        diag_i = kappa * sigma
        inside = soil > 0.0
        size = jnp.where(inside, diag_r * diag_r + diag_i * diag_i, 1.0)
        scale = jnp.where(inside, RELAX_WEIGHT / size, 0.0)
        both, quarter = shear + stiff, 0.25 * stiff
        values = {
            WR: scale * diag_r,
            WI: -scale * diag_i,
            A: shear,
            AB: both,
            H: quarter,
            AM: rolled_zero(shear, 1),
            ABM: rolled_zero(both, 1),
            HM: rolled_zero(quarter, 1),
            AP: rolled_zero(shear, -1),
            ABP: rolled_zero(both, -1),
            HP: rolled_zero(quarter, -1),
        }
        for j, value in values.items():
            coeffs[pl.ds((col * COEFFS + j) * depth, depth), :] = value


def tile_of(col):
    if col < HALO:
        return 0, col
    if col < HALO + WIDTH:
        return 1, col - HALO
    return 2, col - HALO - WIDTH


def pick(which, own, off, on, read):
    if which == 1:
        return read(own)
    even = lax.axis_index("tile") % 2 == 0
    first, second = read(off), read(on)
    return jnp.where(even, first, second) if which == 0 else jnp.where(even, second, first)


def slot(z, col, pc):
    return (z * COLS + col) * PC + pc


def bottom_kernel(shots, depth, layers, first_only, own, off, on, consts, start, *refs):
    bottoms, coeffs, v1, v2 = refs[:WIDTH], *refs[WIDTH:]
    work = functools.partial(
        bottom_planes, shots, depth, layers, own, off, on, consts, start, bottoms, coeffs, v1, v2
    )
    if not first_only:
        work()
        return
    slab = lax.axis_index("slab")
    pl.when(slab == 0)(work)

    @pl.when(slab != 0)
    def _():
        for ref in bottoms:
            ref[...] = jnp.zeros(ref.shape, jnp.float32)


def bottom_planes(shots, depth, layers, own, off, on, consts, start, bottoms, coeffs, v1, v2):
    at = DEEP * WIDTH * PC * shots
    soils = []
    for col in range(COLS):
        which, place = tile_of(col)
        where = pl.ds(at + place * depth, depth)
        soils.append(pick(which, own, off, on, lambda ref: ref[where, :]))
    fill_coeffs(coeffs, soils, consts, depth, layers)
    base = depth - DEEP

    def block(ref, number):
        return ref.at[pl.ds(number * shots, shots), :]

    for z in range(DEEP):
        for col in range(COLS):
            which, place = tile_of(col)
            coef = coef_of(coeffs, col, depth, base + z)
            for c in range(COMPS):
                fr, fi = (
                    pick(which, own, off, on, lambda ref: block(ref, (z * WIDTH + place) * PC + pc)[...])
                    for pc in (c, COMPS + c)
                )
                vr, vi = scaled(fr, fi, coef)
                block(v1, slot(z, col, c))[...] = vr
                block(v1, slot(z, col, COMPS + c))[...] = vi

    def first(x, z, pc):
        return block(v1, slot(z, x, pc))[...] if z < DEEP else None

    def second(x, z, pc):
        return block(v2, slot(z, x, pc))[...] if z < DEEP else None

    for z in range(1, DEEP):
        for x in range(1, COLS - 1):
            got = relaxed(memo(first), first, coef_of(coeffs, x, depth, base + z), x, z)
            for pc in range(PC):
                block(v2, slot(z, x, pc))[...] = got[pc]
    lane = lax.broadcasted_iota(jnp.int32, (shots, 2 * PATCH), 1)
    for x in range(HALO, HALO + WIDTH):
        got = relaxed(memo(second), first, coef_of(coeffs, x, depth, depth - 1), x, DEEP - 1)
        for pair in range(PC // 2):
            even, odd = got[2 * pair], got[2 * pair + 1]
            both = (
                jnp.where(lane < PATCH, even, pltpu.roll(odd, PATCH, 1)),
                jnp.where(lane < PATCH, pltpu.roll(even, PATCH, 1), odd),
            )
            for patch in range(2):
                lanes = pl.ds(pair * 2 * PATCH, 2 * PATCH)
                given = start[pl.ds(((x - HALO) * 2 + patch) * shots, shots), lanes]
                bottoms[x - HALO][pl.ds(patch * shots, shots), lanes] = both[patch] + given


def full_kernel(shots, depth, coeffs, low, low_on, low_off, high, high_off, high_on, out, v1, v2):
    stride = PC * WIDTH * depth
    lows, highs = (low, low_off, low_on), (high, high_off, high_on)
    plane = COLS * PC * shots

    def at(z, col, pc):
        return pl.ds(pl.multiple_of((z + 1) * plane + (col * PC + pc) * shots, shots), shots)

    for ref in (v1, v2):
        for z in (-1, depth):
            for n in range(COLS * PC):
                ref[pl.ds((z + 1) * plane + n * shots, shots), :] = jnp.zeros((shots, 2 * PATCH), jnp.float32)

    def begin(tiles, shift):
        def run(z, carry):
            for col in range(COLS):
                which, place = tile_of(col)
                coef = coef_of(coeffs, col, depth, z)
                for c in range(COMPS):
                    number = ((z - shift) * WIDTH + place) * PC + c
                    fr, fi = (
                        pick(which, *tiles, lambda ref: ref[pl.ds(pl.multiple_of(n * shots, shots), shots), :])
                        for n in (number, number + COMPS)
                    )
                    vr, vi = scaled(fr, fi, coef)
                    v1[at(z, col, c), :] = vr
                    v1[at(z, col, COMPS + c), :] = vi
            return carry

        return run

    lax.fori_loop(0, depth - DEEP, begin(lows, 0), 0)
    lax.fori_loop(depth - DEEP, depth, begin(highs, depth - DEEP), 0)

    def first(x, z, pc):
        return v1[at(z, x, pc), :]

    def second(x, z, pc):
        return v2[at(z, x, pc), :]

    def middle(z, carry):
        for x in range(1, COLS - 1):
            got = relaxed(first, first, coef_of(coeffs, x, depth, z), x, z)
            for pc in range(PC):
                v2[at(z, x, pc), :] = got[pc]
        return carry

    lax.fori_loop(0, depth, middle, 0)

    def last(z, carry):
        for x in range(HALO, HALO + WIDTH):
            got = relaxed(second, first, coef_of(coeffs, x, depth, z), x, z)
            for pc in range(PC):
                out[pl.ds((pc * WIDTH + x - HALO) * depth + z, shots, stride=stride), :] = got[pc]
        return carry

    lax.fori_loop(0, depth, last, 0)


def inject_kernel(shots, depth, offs, coeffs, base, *refs):
    own, traces, halos = refs[:WIDTH], refs[WIDTH : 2 * WIDTH], refs[2 * WIDTH : -4]
    out, whole, v1, v2 = refs[-4:]
    for col, trace in enumerate(traces):
        whole[pl.ds(col * trace.shape[0], trace.shape[0]), :] = trace[...]
    off, on = halos[:offs], halos[offs:]
    stride = PC * WIDTH * depth

    def block(ref, number):
        return ref.at[pl.ds(number * shots, shots), :]

    lane = lax.broadcasted_iota(jnp.int32, (shots, 2 * PATCH), 1)
    for col in range(COLS):
        which, place = tile_of(col)
        coef = coef_of(coeffs, col, depth, 0)
        planes = []
        for pair in range(PC // 2):
            halves = []
            for patch in range(2):
                where = (
                    pl.ds((place * 2 + patch) * shots, shots),
                    pl.ds(pair * 2 * PATCH, 2 * PATCH),
                )
                if which == 1:
                    halves.append(own[place][pl.ds(patch * shots, shots), where[1]])
                else:
                    halves.append(
                        pick(which, None, off, on, lambda refs: plus(*[ref[where] for ref in refs]))
                    )
            planes.append(jnp.where(lane < PATCH, halves[0], pltpu.roll(halves[1], PATCH, 1)))
            planes.append(jnp.where(lane < PATCH, pltpu.roll(halves[0], PATCH, 1), halves[1]))
        shear = coef(A)
        for c in range(COMPS):
            vr, vi = scaled(shear * planes[c], shear * planes[COMPS + c], coef)
            block(v1, slot(0, col, c))[...] = vr
            block(v1, slot(0, col, COMPS + c))[...] = vi

    def first(x, z, pc):
        return block(v1, slot(0, x, pc))[...] if z == 0 else None

    def second(x, z, pc):
        return block(v2, slot(z, x, pc))[...] if 0 <= z < 2 else None

    for z in range(2):
        for x in range(1, COLS - 1):
            got = relaxed(memo(first), first, coef_of(coeffs, x, depth, z), x, z)
            for pc in range(PC):
                block(v2, slot(z, x, pc))[...] = got[pc]
    out[...] = base[...]
    for z in range(3):
        for x in range(HALO, HALO + WIDTH):
            got = relaxed(memo(second), first, coef_of(coeffs, x, depth, z), x, z)
            for pc in range(PC):
                where = (pl.ds((pc * WIDTH + x - HALO) * depth + z, shots, stride=stride), slice(None))
                out[where] = base[where] + got[pc]


def split_kernel(blocks, high, low):
    whole = blocks[...]
    top = whole.astype(jnp.bfloat16)
    high[...] = top
    low[...] = (whole - top.astype(jnp.float32)).astype(jnp.bfloat16)


def product(shots, x, high, low, add, out, first):
    size = x.shape[1]
    for chain in range(x.shape[0] // shots):
        rows = pl.ds(chain * shots, shots)
        whole = x[rows, :]
        top = whole.astype(jnp.bfloat16)
        rest = (whole - top.astype(jnp.float32)).astype(jnp.bfloat16)
        block = pl.ds((first + chain) * size, size)
        wide = jnp.dot(
            jnp.concatenate([top, rest], axis=0), high[block, :], preferred_element_type=jnp.float32
        )
        thin = jnp.dot(top, low[block, :], preferred_element_type=jnp.float32)
        total = wide[:shots] + wide[shots:] + thin
        out[rows, :] = total if add is None else total + add[rows, :]


def start_kernel(shots, inflow, high, low, out, *helds):
    slab = lax.axis_index("slab")

    @pl.when(slab == 0)
    def _():
        product(shots, inflow, high, low, None, out, 0)

    @pl.when(slab != 0)
    def _():
        out[...] = jnp.zeros(out.shape, jnp.float32)

    for col, ref in enumerate(helds):
        ref[...] = inflow[pl.ds(col * ref.shape[0], ref.shape[0]), :]


def hop_kernel(shots, turn, col, groups, *refs):
    arrived, high, low, bottom, trace, held, *rest = refs
    sides, (new_trace, new_held, *sums) = rest[: sum(groups)], rest[sum(groups) :]
    slab = lax.axis_index("slab")

    @pl.when(slab == turn)
    def _():
        product(shots, arrived, high, low, bottom, new_trace, col * (arrived.shape[0] // shots))
        new_held[...] = arrived[...]

    @pl.when(slab != turn)
    def _():
        new_trace[...] = trace[...]
        new_held[...] = held[...]

    for ref, count in zip(sums, [g for g in groups if g]):
        ref[...] = plus(*[side[...] for side in sides[:count]])
        sides = sides[count:]


def gather_kernel(turn, *refs):
    mine, rows = refs[-1], refs[0].shape[0]
    traces, helds = refs[:WIDTH], refs[WIDTH:-1]

    def fill(parts):
        for number, part in enumerate(parts):
            mine[pl.ds(number * rows, rows), :] = part[...]

    slab = lax.axis_index("slab")
    pl.when(slab == turn)(lambda: fill(traces))
    pl.when(slab != turn)(lambda: fill(helds))


def per_device(source, soil_index, soil_table, pml_width, interface_blocks, inflow):
    shots, _, _, width, depth, length = source.shape
    layers = soil_table.shape[1]
    size = interface_blocks.shape[-1]
    slabs, tiles = lax.axis_size("slab"), lax.axis_size("tile")
    f32, bf16 = jnp.float32, jnp.bfloat16
    chains = width * (length // PATCH)
    low_rows = (depth - DEEP) * width * PC * shots
    high_rows = DEEP * width * PC * shots + width * depth

    off = [p for t in range(1, tiles - 1, 2) for p in ((t, t + 1), (t + 1, t))]
    on = [p for t in range(0, tiles - 1, 2) for p in ((t, t + 1), (t + 1, t))]

    def pairs(slab_moves, tile_moves):
        return [(a * tiles + t, b * tiles + u) for a, b in slab_moves for t, u in tile_moves]

    def both(x, moves):
        return lax.ppermute(x, ("slab", "tile"), moves)

    src, soil = source.reshape(-1, length), soil_index.reshape(-1, length)
    (high,) = call(
        "pack_high",
        functools.partial(pack_high_kernel, shots, depth),
        [((high_rows, length), f32)],
        [pltpu.with_memory_space_constraint(x, pltpu.HBM) for x in (src, soil)],
        [ANY, ANY],
        [
            pltpu.VMEM(src.shape, f32),
            pltpu.VMEM(soil.shape, jnp.int32),
            pltpu.SemaphoreType.DMA((2,)),
        ],
    )
    high_off, high_on = lax.ppermute(high, "tile", off), lax.ppermute(high, "tile", on)

    blocks = interface_blocks.reshape(chains * size, size)
    heavy, light = call("split", split_kernel, [(blocks.shape, bf16)] * 2, [blocks])
    held = inflow.reshape(chains * shots, size)
    row_shape = ((chains * shots, size), f32)
    chunk = (chains // width * shots, size)
    start, *helds = call(
        "start",
        functools.partial(start_kernel, shots),
        [row_shape] + [(chunk, f32)] * width,
        [held, heavy, light],
    )
    table_shape = (COLS * COEFFS * depth, length)
    planes = [pltpu.VMEM((DEEP * COLS * PC * shots, length), f32)] * 2
    (consts,) = call(
        "consts",
        functools.partial(consts_kernel, depth, layers),
        [((depth + 3 * layers, length), f32)],
        [soil_table, pml_width],
        [SMEM, SMEM],
    )
    near = [high, high_off, high_on, consts, start]
    traces = call(
        "first",
        functools.partial(bottom_kernel, shots, depth, layers, True),
        [(chunk, f32)] * width,
        near,
        None,
        [pltpu.VMEM(table_shape, f32)] + planes,
    )
    *bottoms, coeffs = call(
        "bottom",
        functools.partial(bottom_kernel, shots, depth, layers, False),
        [(chunk, f32)] * width + [(table_shape, f32)],
        near,
        None,
        planes,
        flops=HOP_COST,
    )
    offs, ons = [], []
    first_far, mine = slabs // 2, None
    for hop in range(slabs - 1):
        step = pairs([(hop, hop + 1)], [(t, t) for t in range(tiles)])
        arrived = [both(trace, step) for trace in traces]
        groups = (len(offs), len(ons))
        sides = [*offs, *ons]
        if hop in (1, slabs - 2):
            arrived = lax.optimization_barrier(arrived)
        from_off, from_on = [], []
        if hop >= first_far:
            same = range(hop) if hop == first_far else [first_far] if hop == first_far + 1 else []
            from_off = [both(mine, pairs([(hop, hop + 1)] + [(s, s) for s in same], off))]
        if hop == slabs - 2:
            (entered,) = call(
                "entered",
                functools.partial(gather_kernel, hop + 1),
                [row_shape],
                [*arrived, *helds],
                flops=GATHER_COST,
            )
            from_on = [lax.ppermute(entered, "tile", on)]
        if hop == 1:
            again, _ = lax.optimization_barrier((src, traces))
            (low,) = call(
                "pack_low",
                functools.partial(pack_low_kernel, shots, depth),
                [((low_rows, length), f32)],
                [again],
                flops=LOW_COST,
            )
            low_on, low_off = lax.ppermute(low, "tile", on), lax.ppermute(low, "tile", off)
        if hop == first_far - 1:
            lows, _ = lax.optimization_barrier(((low, low_on, low_off), traces))
            (solved,) = call(
                "full",
                functools.partial(full_kernel, shots, depth),
                [((shots * PC * width * depth, length), f32)],
                [coeffs, *lows, high, high_off, high_on],
                None,
                [pltpu.VMEM(((depth + 2) * COLS * PC * shots, length), f32)] * 2,
                flops=FULL_COST,
                limit=12 * MIB,
            )
            arrived[-1], solved = lax.optimization_barrier((arrived[-1], solved))
        sums = []
        new_traces, new_helds = [None] * width, [None] * width
        for col in reversed(range(width)):
            if hop == first_far - 1 and col < width - 1:
                arrived[col], _ = lax.optimization_barrier((arrived[col], new_traces[-1]))
            counts = groups if col == width - 1 else (0, 0)
            new_traces[col], new_helds[col], *more = call(
                f"hop{hop}_{col}",
                functools.partial(hop_kernel, shots, hop + 1, col, counts),
                [(chunk, f32)] * 2 + [row_shape] * sum(c > 0 for c in counts),
                [arrived[col], heavy, light, bottoms[col], traces[col], helds[col]]
                + (sides if col == width - 1 else []),
                flops=HOP_COSTS[hop],
            )
            sums = more or sums
        traces, helds = new_traces, new_helds
        if first_far - 1 <= hop < slabs - 2:
            (mine,) = call(
                f"gather{hop}",
                functools.partial(gather_kernel, hop + 1),
                [row_shape],
                [*traces, *helds],
                flops=GATHER_COST,
            )
        offs = ([sums.pop(0)] if groups[0] else []) + from_off
        ons = ([sums.pop(0)] if groups[1] else []) + from_on
    result, whole = call(
        "inject",
        functools.partial(inject_kernel, shots, depth, len(offs)),
        [(solved.shape, f32), row_shape],
        [coeffs, solved, *helds, *traces, *offs, *ons],
        None,
        planes,
    )
    traces = whole.reshape(width, 1, length // PATCH, shots, size)
    return result.reshape(source.shape), traces


def solution(mesh):
    in_specs = (
        P(None, None, None, "tile", "slab", None),
        P("tile", "slab", None),
        P(),
        P("slab", None),
        P("tile", "slab", None, None, None),
        P("tile", None, None, None),
    )
    out_specs = (P(None, None, None, "tile", "slab", None), P("tile", "slab", None, None, None))
    return jax.shard_map(
        per_device, mesh=mesh, in_specs=in_specs, out_specs=out_specs, check_vma=False
    )
```

```python
import functools

import jax
import jax.numpy as jnp
from jax import lax
from jax.experimental import pallas as pl
import jax.experimental.pallas.tpu as pltpu
from jax.sharding import PartitionSpec as P

PATCH = 64
RELAX_WEIGHT = 0.8
SIGMA_PEAK = 3.0
PARTS, COMPS = 2, 3
PC = PARTS * COMPS
WIDTH = 2
HALO = 2
COLS = WIDTH + 2 * HALO
DEEP = 3
COEFFS = 11
WR, WI, A, AB, H, AM, ABM, HM, AP, ABP, HP = range(COEFFS)
VMEM = pl.BlockSpec(memory_space=pltpu.VMEM)
SMEM = pl.BlockSpec(memory_space=pltpu.SMEM)
ANY = pl.BlockSpec(memory_space=pl.ANY)
MIB = 1024 * 1024
LIMIT = 6 * MIB
HOP_COST = 2e9
LOW_COST = 2e9
HOP_COSTS = (2e9, 2e9, 2e9, 2e9, 1e6, 1e6, 2e9)
GATHER_COST = 2e9
FULL_COST = 5e9


def call(name, body, outs, operands, specs=None, scratch=(), flops=5e8, limit=LIMIT):
    return pl.pallas_call(
        body,
        name=name,
        out_shape=[jax.ShapeDtypeStruct(shape, dtype) for shape, dtype in outs],
        in_specs=specs or [VMEM] * len(operands),
        out_specs=[VMEM] * len(outs),
        scratch_shapes=list(scratch),
        compiler_params=pltpu.CompilerParams(vmem_limit_bytes=limit),
        cost_estimate=pl.CostEstimate(flops=int(flops), bytes_accessed=0, transcendentals=0),
    )(*operands)


def put(src, target, shots, depth, d, col, pc, place):
    stride = PC * WIDTH * depth
    rows = src[pl.ds((pc * WIDTH + col) * depth + d, shots, stride=stride), :]
    target[pl.ds(((place * WIDTH + col) * PC + pc) * shots, shots), :] = rows


def pack_high_kernel(shots, depth, src_hbm, soil_hbm, high, src, soil, sems):
    copies = (
        pltpu.make_async_copy(src_hbm, src, sems.at[0]),
        pltpu.make_async_copy(soil_hbm, soil, sems.at[1]),
    )
    for copy in copies:
        copy.start()
    for copy in copies:
        copy.wait()
    for place in range(DEEP):
        for col in range(WIDTH):
            for pc in range(PC):
                put(src, high, shots, depth, depth - DEEP + place, col, pc, place)
    tail = pl.ds(DEEP * WIDTH * PC * shots, WIDTH * depth)
    high[tail, :] = (soil[...] + 1).astype(jnp.float32)


def pack_low_kernel(shots, depth, src, low):
    for d in range(depth - DEEP):
        for col in range(WIDTH):
            for pc in range(PC):
                put(src, low, shots, depth, d, col, pc, d)


def plus(*terms):
    terms = [t for t in terms if t is not None]
    return functools.reduce(lambda a, b: a + b, terms) if terms else None


def minus(a, b):
    if b is None:
        return a
    return -b if a is None else a - b


def times(c, a):
    return None if a is None else c * a


def coupling(field, coef, x, z):
    def step(c):
        return minus(field(x + 1, z, c), field(x - 1, z, c))

    def dive(col, c):
        return minus(field(col, z + 1, c), field(col, z - 1, c))

    def sides(c):
        return plus(field(x + 1, z, c), field(x - 1, z, c))

    def ends(c):
        return plus(field(x, z + 1, c), field(x, z - 1, c))

    length = 128
    results = []
    for c in range(COMPS):
        own = field(x, z, c)
        if c == 0:
            total = plus(
                times(coef(AB), sides(0)),
                times(coef(A), ends(0)),
                times(coef(H), minus(dive(x + 1, 2), dive(x - 1, 2))),
            )
            cross = step(1)
        elif c == 1:
            total = times(coef(A), plus(sides(1), ends(1)))
            cross = plus(step(0), dive(x, 2))
        else:
            total = plus(
                times(coef(A), sides(2)),
                times(coef(AB), ends(2)),
                times(coef(H), minus(dive(x + 1, 0), dive(x - 1, 0))),
            )
            cross = dive(x, 1)
        before, after = (ABM, ABP) if c == 1 else (AM, AP)
        ahead = plus(times(coef(before), own), times(coef(HM), cross))
        behind = minus(times(coef(after), own), times(coef(HP), cross))
        if ahead is not None:
            total = plus(total, pltpu.roll(ahead, length - 1, 1), pltpu.roll(behind, 1, 1))
        results.append(total)
    return results


def relaxed(field, first, coef, x, z):
    real = coupling(lambda i, k, c: field(i, k, c), coef, x, z)
    imag = coupling(lambda i, k, c: field(i, k, COMPS + c), coef, x, z)
    wr, wi = coef(WR), coef(WI)
    out = []
    for part in range(PARTS):
        for c in range(COMPS):
            pc = part * COMPS + c
            if part == 0:
                update = minus(times(wr, real[c]), times(wi, imag[c]))
            else:
                update = plus(times(wr, imag[c]), times(wi, real[c]))
            out.append(plus(times(1.0 - RELAX_WEIGHT, field(x, z, pc)), first(x, z, pc), update))
    return out


def scaled(fr, fi, coef):
    wr, wi = coef(WR), coef(WI)
    return wr * fr - wi * fi, wr * fi + wi * fr


def memo(fn):
    cache = {}

    def get(*key):
        if key not in cache:
            cache[key] = fn(*key)
        return cache[key]

    return get


def coef_of(coeffs, col, depth, z):
    return memo(lambda j: coeffs[pl.ds((col * COEFFS + j) * depth + z, 1), :])


def rolled_zero(x, shift):
    lane = lax.broadcasted_iota(jnp.int32, x.shape, 1)
    length = x.shape[1]
    if shift == 1:
        return jnp.where(lane == 0, 0.0, pltpu.roll(x, 1, 1))
    return jnp.where(lane == length - 1, 0.0, pltpu.roll(x, length - 1, 1))


def consts_kernel(depth, layers, table, widths, out):
    shape = (depth, out.shape[1])
    level = lax.broadcasted_iota(jnp.int32, shape, 0)
    top, bottom = widths[0, 0], widths[0, 1]
    zero = jnp.zeros(shape, jnp.int32)
    upper = jnp.maximum(top - level, 0).astype(jnp.float32) / (zero + top).astype(jnp.float32)
    lower = jnp.maximum(bottom - (depth - 1 - level), 0).astype(jnp.float32) / (
        zero + bottom
    ).astype(jnp.float32)
    out[pl.ds(0, depth), :] = SIGMA_PEAK * upper * upper + SIGMA_PEAK * lower * lower
    for row in range(3):
        for layer in range(layers):
            value = jnp.full((1, out.shape[1]), table[row, layer], jnp.float32)
            out[pl.ds(depth + row * layers + layer, 1), :] = value


def fill_coeffs(coeffs, soils, consts, depth, layers):
    shape = soils[0].shape
    sigma = consts[pl.ds(0, depth), :]
    for col, soil in enumerate(soils):
        rows = []
        for row in range(3):
            picked = jnp.zeros(shape, jnp.float32)
            for layer in range(layers):
                value = consts[pl.ds(depth + row * layers + layer, 1), :]
                picked = jnp.where(soil == layer + 1.0, value, picked)
            rows.append(picked)
        shear, lame, kappa = rows
        stiff = lame + shear
        diag_r = 6.0 * shear + 2.0 * stiff + kappa
        diag_i = kappa * sigma
        inside = soil > 0.0
        size = jnp.where(inside, diag_r * diag_r + diag_i * diag_i, 1.0)
        scale = jnp.where(inside, RELAX_WEIGHT / size, 0.0)
        both, quarter = shear + stiff, 0.25 * stiff
        values = {
            WR: scale * diag_r,
            WI: -scale * diag_i,
            A: shear,
            AB: both,
            H: quarter,
            AM: rolled_zero(shear, 1),
            ABM: rolled_zero(both, 1),
            HM: rolled_zero(quarter, 1),
            AP: rolled_zero(shear, -1),
            ABP: rolled_zero(both, -1),
            HP: rolled_zero(quarter, -1),
        }
        for j, value in values.items():
            coeffs[pl.ds((col * COEFFS + j) * depth, depth), :] = value


def tile_of(col):
    if col < HALO:
        return 0, col
    if col < HALO + WIDTH:
        return 1, col - HALO
    return 2, col - HALO - WIDTH


def pick(which, own, off, on, read):
    if which == 1:
        return read(own)
    even = lax.axis_index("tile") % 2 == 0
    first, second = read(off), read(on)
    return jnp.where(even, first, second) if which == 0 else jnp.where(even, second, first)


def slot(z, col, pc):
    return (z * COLS + col) * PC + pc


def bottom_kernel(shots, depth, layers, first_only, own, off, on, consts, start, *refs):
    bottoms, coeffs, v1, v2 = refs[:WIDTH], *refs[WIDTH:]
    work = functools.partial(
        bottom_planes, shots, depth, layers, own, off, on, consts, start, bottoms, coeffs, v1, v2
    )
    if not first_only:
        work()
        return
    slab = lax.axis_index("slab")
    pl.when(slab == 0)(work)

    @pl.when(slab != 0)
    def _():
        for ref in bottoms:
            ref[...] = jnp.zeros(ref.shape, jnp.float32)


def bottom_planes(shots, depth, layers, own, off, on, consts, start, bottoms, coeffs, v1, v2):
    at = DEEP * WIDTH * PC * shots
    soils = []
    for col in range(COLS):
        which, place = tile_of(col)
        where = pl.ds(at + place * depth, depth)
        soils.append(pick(which, own, off, on, lambda ref: ref[where, :]))
    fill_coeffs(coeffs, soils, consts, depth, layers)
    base = depth - DEEP

    def block(ref, number):
        return ref.at[pl.ds(number * shots, shots), :]

    for z in range(DEEP):
        for col in range(COLS):
            which, place = tile_of(col)
            coef = coef_of(coeffs, col, depth, base + z)
            for c in range(COMPS):
                fr, fi = (
                    pick(which, own, off, on, lambda ref: block(ref, (z * WIDTH + place) * PC + pc)[...])
                    for pc in (c, COMPS + c)
                )
                vr, vi = scaled(fr, fi, coef)
                block(v1, slot(z, col, c))[...] = vr
                block(v1, slot(z, col, COMPS + c))[...] = vi

    def first(x, z, pc):
        return block(v1, slot(z, x, pc))[...] if z < DEEP else None

    def second(x, z, pc):
        return block(v2, slot(z, x, pc))[...] if z < DEEP else None

    for z in range(1, DEEP):
        for x in range(1, COLS - 1):
            got = relaxed(memo(first), first, coef_of(coeffs, x, depth, base + z), x, z)
            for pc in range(PC):
                block(v2, slot(z, x, pc))[...] = got[pc]
    lane = lax.broadcasted_iota(jnp.int32, (shots, 2 * PATCH), 1)
    for x in range(HALO, HALO + WIDTH):
        got = relaxed(memo(second), first, coef_of(coeffs, x, depth, depth - 1), x, DEEP - 1)
        for pair in range(PC // 2):
            even, odd = got[2 * pair], got[2 * pair + 1]
            both = (
                jnp.where(lane < PATCH, even, pltpu.roll(odd, PATCH, 1)),
                jnp.where(lane < PATCH, pltpu.roll(even, PATCH, 1), odd),
            )
            for patch in range(2):
                lanes = pl.ds(pair * 2 * PATCH, 2 * PATCH)
                given = start[pl.ds(((x - HALO) * 2 + patch) * shots, shots), lanes]
                bottoms[x - HALO][pl.ds(patch * shots, shots), lanes] = both[patch] + given


def full_kernel(shots, depth, coeffs, low, low_off, low_on, high, high_off, high_on, out, v1, v2):
    stride = PC * WIDTH * depth
    lows, highs = (low, low_off, low_on), (high, high_off, high_on)
    plane = COLS * PC * shots

    def at(z, col, pc):
        return pl.ds(pl.multiple_of((z + 1) * plane + (col * PC + pc) * shots, shots), shots)

    for ref in (v1, v2):
        for z in (-1, depth):
            for n in range(COLS * PC):
                ref[pl.ds((z + 1) * plane + n * shots, shots), :] = jnp.zeros((shots, 2 * PATCH), jnp.float32)

    def begin(tiles, shift):
        def run(z, carry):
            for col in range(COLS):
                which, place = tile_of(col)
                coef = coef_of(coeffs, col, depth, z)
                for c in range(COMPS):
                    number = ((z - shift) * WIDTH + place) * PC + c
                    fr, fi = (
                        pick(which, *tiles, lambda ref: ref[pl.ds(pl.multiple_of(n * shots, shots), shots), :])
                        for n in (number, number + COMPS)
                    )
                    vr, vi = scaled(fr, fi, coef)
                    v1[at(z, col, c), :] = vr
                    v1[at(z, col, COMPS + c), :] = vi
            return carry

        return run

    lax.fori_loop(0, depth - DEEP, begin(lows, 0), 0)
    lax.fori_loop(depth - DEEP, depth, begin(highs, depth - DEEP), 0)

    def first(x, z, pc):
        return v1[at(z, x, pc), :]

    def second(x, z, pc):
        return v2[at(z, x, pc), :]

    def middle(z, carry):
        for x in range(1, COLS - 1):
            got = relaxed(first, first, coef_of(coeffs, x, depth, z), x, z)
            for pc in range(PC):
                v2[at(z, x, pc), :] = got[pc]
        return carry

    lax.fori_loop(0, depth, middle, 0)

    def last(z, carry):
        for x in range(HALO, HALO + WIDTH):
            got = relaxed(second, first, coef_of(coeffs, x, depth, z), x, z)
            for pc in range(PC):
                out[pl.ds((pc * WIDTH + x - HALO) * depth + z, shots, stride=stride), :] = got[pc]
        return carry

    lax.fori_loop(0, depth, last, 0)


def inject_kernel(shots, depth, offs, coeffs, base, *refs):
    own, traces, halos = refs[:WIDTH], refs[WIDTH : 2 * WIDTH], refs[2 * WIDTH : -4]
    out, whole, v1, v2 = refs[-4:]
    for col, trace in enumerate(traces):
        whole[pl.ds(col * trace.shape[0], trace.shape[0]), :] = trace[...]
    off, on = halos[:offs], halos[offs:]
    stride = PC * WIDTH * depth

    def block(ref, number):
        return ref.at[pl.ds(number * shots, shots), :]

    lane = lax.broadcasted_iota(jnp.int32, (shots, 2 * PATCH), 1)
    for col in range(COLS):
        which, place = tile_of(col)
        coef = coef_of(coeffs, col, depth, 0)
        planes = []
        for pair in range(PC // 2):
            halves = []
            for patch in range(2):
                where = (
                    pl.ds((place * 2 + patch) * shots, shots),
                    pl.ds(pair * 2 * PATCH, 2 * PATCH),
                )
                if which == 1:
                    halves.append(own[place][pl.ds(patch * shots, shots), where[1]])
                else:
                    halves.append(
                        pick(which, None, off, on, lambda refs: plus(*[ref[where] for ref in refs]))
                    )
            planes.append(jnp.where(lane < PATCH, halves[0], pltpu.roll(halves[1], PATCH, 1)))
            planes.append(jnp.where(lane < PATCH, pltpu.roll(halves[0], PATCH, 1), halves[1]))
        shear = coef(A)
        for c in range(COMPS):
            vr, vi = scaled(shear * planes[c], shear * planes[COMPS + c], coef)
            block(v1, slot(0, col, c))[...] = vr
            block(v1, slot(0, col, COMPS + c))[...] = vi

    def first(x, z, pc):
        return block(v1, slot(0, x, pc))[...] if z == 0 else None

    def second(x, z, pc):
        return block(v2, slot(z, x, pc))[...] if 0 <= z < 2 else None

    for z in range(2):
        for x in range(1, COLS - 1):
            got = relaxed(memo(first), first, coef_of(coeffs, x, depth, z), x, z)
            for pc in range(PC):
                block(v2, slot(z, x, pc))[...] = got[pc]
    out[...] = base[...]
    for z in range(3):
        for x in range(HALO, HALO + WIDTH):
            got = relaxed(memo(second), first, coef_of(coeffs, x, depth, z), x, z)
            for pc in range(PC):
                where = (pl.ds((pc * WIDTH + x - HALO) * depth + z, shots, stride=stride), slice(None))
                out[where] = base[where] + got[pc]


def split_kernel(blocks, high, low):
    whole = blocks[...]
    top = whole.astype(jnp.bfloat16)
    high[...] = top
    low[...] = (whole - top.astype(jnp.float32)).astype(jnp.bfloat16)


def product(shots, x, high, low, add, out, first):
    size = x.shape[1]
    for chain in range(x.shape[0] // shots):
        rows = pl.ds(chain * shots, shots)
        whole = x[rows, :]
        top = whole.astype(jnp.bfloat16)
        rest = (whole - top.astype(jnp.float32)).astype(jnp.bfloat16)
        block = pl.ds((first + chain) * size, size)
        wide = jnp.dot(
            jnp.concatenate([top, rest], axis=0), high[block, :], preferred_element_type=jnp.float32
        )
        thin = jnp.dot(top, low[block, :], preferred_element_type=jnp.float32)
        total = wide[:shots] + wide[shots:] + thin
        out[rows, :] = total if add is None else total + add[rows, :]


def start_kernel(shots, inflow, high, low, out, *helds):
    slab = lax.axis_index("slab")

    @pl.when(slab == 0)
    def _():
        product(shots, inflow, high, low, None, out, 0)

    @pl.when(slab != 0)
    def _():
        out[...] = jnp.zeros(out.shape, jnp.float32)

    for col, ref in enumerate(helds):
        ref[...] = inflow[pl.ds(col * ref.shape[0], ref.shape[0]), :]


def hop_kernel(shots, turn, col, groups, *refs):
    arrived, high, low, bottom, trace, held, *rest = refs
    sides, (new_trace, new_held, *sums) = rest[: sum(groups)], rest[sum(groups) :]
    slab = lax.axis_index("slab")

    @pl.when(slab == turn)
    def _():
        product(shots, arrived, high, low, bottom, new_trace, col * (arrived.shape[0] // shots))
        new_held[...] = arrived[...]

    @pl.when(slab != turn)
    def _():
        new_trace[...] = trace[...]
        new_held[...] = held[...]

    for ref, count in zip(sums, [g for g in groups if g]):
        ref[...] = plus(*[side[...] for side in sides[:count]])
        sides = sides[count:]


def gather_kernel(turn, *refs):
    mine, rows = refs[-1], refs[0].shape[0]
    traces, helds = refs[:WIDTH], refs[WIDTH:-1]

    def fill(parts):
        for number, part in enumerate(parts):
            mine[pl.ds(number * rows, rows), :] = part[...]

    slab = lax.axis_index("slab")
    pl.when(slab == turn)(lambda: fill(traces))
    pl.when(slab != turn)(lambda: fill(helds))


def per_device(source, soil_index, soil_table, pml_width, interface_blocks, inflow):
    shots, _, _, width, depth, length = source.shape
    layers = soil_table.shape[1]
    size = interface_blocks.shape[-1]
    slabs, tiles = lax.axis_size("slab"), lax.axis_size("tile")
    f32, bf16 = jnp.float32, jnp.bfloat16
    chains = width * (length // PATCH)
    low_rows = (depth - DEEP) * width * PC * shots
    high_rows = DEEP * width * PC * shots + width * depth

    off = [p for t in range(1, tiles - 1, 2) for p in ((t, t + 1), (t + 1, t))]
    on = [p for t in range(0, tiles - 1, 2) for p in ((t, t + 1), (t + 1, t))]

    def pairs(slab_moves, tile_moves):
        return [(a * tiles + t, b * tiles + u) for a, b in slab_moves for t, u in tile_moves]

    def both(x, moves):
        return lax.ppermute(x, ("slab", "tile"), moves)

    src, soil = source.reshape(-1, length), soil_index.reshape(-1, length)
    (high,) = call(
        "pack_high",
        functools.partial(pack_high_kernel, shots, depth),
        [((high_rows, length), f32)],
        [pltpu.with_memory_space_constraint(x, pltpu.HBM) for x in (src, soil)],
        [ANY, ANY],
        [
            pltpu.VMEM(src.shape, f32),
            pltpu.VMEM(soil.shape, jnp.int32),
            pltpu.SemaphoreType.DMA((2,)),
        ],
    )
    high_off, high_on = lax.ppermute(high, "tile", off), lax.ppermute(high, "tile", on)

    blocks = interface_blocks.reshape(chains * size, size)
    heavy, light = call("split", split_kernel, [(blocks.shape, bf16)] * 2, [blocks])
    held = inflow.reshape(chains * shots, size)
    row_shape = ((chains * shots, size), f32)
    chunk = (chains // width * shots, size)
    start, *helds = call(
        "start",
        functools.partial(start_kernel, shots),
        [row_shape] + [(chunk, f32)] * width,
        [held, heavy, light],
    )
    table_shape = (COLS * COEFFS * depth, length)
    planes = [pltpu.VMEM((DEEP * COLS * PC * shots, length), f32)] * 2
    (consts,) = call(
        "consts",
        functools.partial(consts_kernel, depth, layers),
        [((depth + 3 * layers, length), f32)],
        [soil_table, pml_width],
        [SMEM, SMEM],
    )
    near = [high, high_off, high_on, consts, start]
    traces = call(
        "first",
        functools.partial(bottom_kernel, shots, depth, layers, True),
        [(chunk, f32)] * width,
        near,
        None,
        [pltpu.VMEM(table_shape, f32)] + planes,
    )
    *bottoms, coeffs = call(
        "bottom",
        functools.partial(bottom_kernel, shots, depth, layers, False),
        [(chunk, f32)] * width + [(table_shape, f32)],
        near,
        None,
        planes,
        flops=HOP_COST,
    )
    offs, ons = [], []
    first_far, mine = slabs // 2, None
    for hop in range(slabs - 1):
        step = pairs([(hop, hop + 1)], [(t, t) for t in range(tiles)])
        arrived = [both(trace, step) for trace in traces]
        groups = (len(offs), len(ons))
        sides = [*offs, *ons]
        if hop in (1, slabs - 2):
            arrived = lax.optimization_barrier(arrived)
        from_off, from_on = [], []
        if hop >= first_far:
            same = range(hop) if hop == first_far else [first_far] if hop == first_far + 1 else []
            from_off = [both(mine, pairs([(hop, hop + 1)] + [(s, s) for s in same], off))]
        if hop == slabs - 2:
            (entered,) = call(
                "entered",
                functools.partial(gather_kernel, hop + 1),
                [row_shape],
                [*arrived, *helds],
                flops=GATHER_COST,
            )
            from_on = [lax.ppermute(entered, "tile", on)]
        if hop == 1:
            again, _ = lax.optimization_barrier((src, traces))
            (low,) = call(
                "pack_low",
                functools.partial(pack_low_kernel, shots, depth),
                [((low_rows, length), f32)],
                [again],
                flops=LOW_COST,
            )
            low_off, low_on = lax.ppermute(low, "tile", off), lax.ppermute(low, "tile", on)
        if hop == first_far - 1:
            lows, _ = lax.optimization_barrier(((low, low_off, low_on), traces))
            (solved,) = call(
                "full",
                functools.partial(full_kernel, shots, depth),
                [((shots * PC * width * depth, length), f32)],
                [coeffs, *lows, high, high_off, high_on],
                None,
                [pltpu.VMEM(((depth + 2) * COLS * PC * shots, length), f32)] * 2,
                flops=FULL_COST,
                limit=12 * MIB,
            )
            arrived[-1], solved = lax.optimization_barrier((arrived[-1], solved))
        sums = []
        new_traces, new_helds = [None] * width, [None] * width
        for col in reversed(range(width)):
            if hop == first_far - 1 and col < width - 1:
                arrived[col], _ = lax.optimization_barrier((arrived[col], new_traces[-1]))
            counts = groups if col == width - 1 else (0, 0)
            new_traces[col], new_helds[col], *more = call(
                f"hop{hop}_{col}",
                functools.partial(hop_kernel, shots, hop + 1, col, counts),
                [(chunk, f32)] * 2 + [row_shape] * sum(c > 0 for c in counts),
                [arrived[col], heavy, light, bottoms[col], traces[col], helds[col]]
                + (sides if col == width - 1 else []),
                flops=HOP_COSTS[hop],
            )
            sums = more or sums
        traces, helds = new_traces, new_helds
        if first_far - 1 <= hop < slabs - 2:
            (mine,) = call(
                f"gather{hop}",
                functools.partial(gather_kernel, hop + 1),
                [row_shape],
                [*traces, *helds],
                flops=GATHER_COST,
            )
        offs = ([sums.pop(0)] if groups[0] else []) + from_off
        ons = ([sums.pop(0)] if groups[1] else []) + from_on
    result, whole = call(
        "inject",
        functools.partial(inject_kernel, shots, depth, len(offs)),
        [(solved.shape, f32), row_shape],
        [coeffs, solved, *helds, *traces, *offs, *ons],
        None,
        planes,
    )
    traces = whole.reshape(width, 1, length // PATCH, shots, size)
    return result.reshape(source.shape), traces


def solution(mesh):
    in_specs = (
        P(None, None, None, "tile", "slab", None),
        P("tile", "slab", None),
        P(),
        P("slab", None),
        P("tile", "slab", None, None, None),
        P("tile", None, None, None),
    )
    out_specs = (P(None, None, None, "tile", "slab", None), P("tile", "slab", None, None, None))
    return jax.shard_map(
        per_device, mesh=mesh, in_specs=in_specs, out_specs=out_specs, check_vma=False
    )
```

```python
import functools

import jax
import jax.numpy as jnp
from jax import lax
from jax.experimental import pallas as pl
import jax.experimental.pallas.tpu as pltpu
from jax.sharding import PartitionSpec as P

PATCH = 64
RELAX_WEIGHT = 0.8
SIGMA_PEAK = 3.0
PARTS, COMPS = 2, 3
PC = PARTS * COMPS
WIDTH = 2
HALO = 2
COLS = WIDTH + 2 * HALO
DEEP = 3
COEFFS = 11
WR, WI, A, AB, H, AM, ABM, HM, AP, ABP, HP = range(COEFFS)
VMEM = pl.BlockSpec(memory_space=pltpu.VMEM)
SMEM = pl.BlockSpec(memory_space=pltpu.SMEM)
ANY = pl.BlockSpec(memory_space=pl.ANY)
MIB = 1024 * 1024
LIMIT = 6 * MIB
HOP_COST = 2e9
LOW_COST = 2e9
HOP_COSTS = (2e9, 4e9, 4e9, 2e9, 1e6, 1e6, 2e9)
GATHER_COST = 2e9
FULL_COST = 5e9


def call(name, body, outs, operands, specs=None, scratch=(), flops=5e8, limit=LIMIT):
    return pl.pallas_call(
        body,
        name=name,
        out_shape=[jax.ShapeDtypeStruct(shape, dtype) for shape, dtype in outs],
        in_specs=specs or [VMEM] * len(operands),
        out_specs=[VMEM] * len(outs),
        scratch_shapes=list(scratch),
        compiler_params=pltpu.CompilerParams(vmem_limit_bytes=limit),
        cost_estimate=pl.CostEstimate(flops=int(flops), bytes_accessed=0, transcendentals=0),
    )(*operands)


def put(src, target, shots, depth, d, col, pc, place):
    stride = PC * WIDTH * depth
    rows = src[pl.ds((pc * WIDTH + col) * depth + d, shots, stride=stride), :]
    target[pl.ds(((place * WIDTH + col) * PC + pc) * shots, shots), :] = rows


def pack_high_kernel(shots, depth, src_hbm, soil_hbm, high, src, soil, sems):
    copies = (
        pltpu.make_async_copy(src_hbm, src, sems.at[0]),
        pltpu.make_async_copy(soil_hbm, soil, sems.at[1]),
    )
    for copy in copies:
        copy.start()
    for copy in copies:
        copy.wait()
    for place in range(DEEP):
        for col in range(WIDTH):
            for pc in range(PC):
                put(src, high, shots, depth, depth - DEEP + place, col, pc, place)
    tail = pl.ds(DEEP * WIDTH * PC * shots, WIDTH * depth)
    high[tail, :] = (soil[...] + 1).astype(jnp.float32)


def pack_low_kernel(shots, depth, src, low):
    for d in range(depth - DEEP):
        for col in range(WIDTH):
            for pc in range(PC):
                put(src, low, shots, depth, d, col, pc, d)


def plus(*terms):
    terms = [t for t in terms if t is not None]
    return functools.reduce(lambda a, b: a + b, terms) if terms else None


def minus(a, b):
    if b is None:
        return a
    return -b if a is None else a - b


def times(c, a):
    return None if a is None else c * a


def coupling(field, coef, x, z):
    def step(c):
        return minus(field(x + 1, z, c), field(x - 1, z, c))

    def dive(col, c):
        return minus(field(col, z + 1, c), field(col, z - 1, c))

    def sides(c):
        return plus(field(x + 1, z, c), field(x - 1, z, c))

    def ends(c):
        return plus(field(x, z + 1, c), field(x, z - 1, c))

    length = 128
    results = []
    for c in range(COMPS):
        own = field(x, z, c)
        if c == 0:
            total = plus(
                times(coef(AB), sides(0)),
                times(coef(A), ends(0)),
                times(coef(H), minus(dive(x + 1, 2), dive(x - 1, 2))),
            )
            cross = step(1)
        elif c == 1:
            total = times(coef(A), plus(sides(1), ends(1)))
            cross = plus(step(0), dive(x, 2))
        else:
            total = plus(
                times(coef(A), sides(2)),
                times(coef(AB), ends(2)),
                times(coef(H), minus(dive(x + 1, 0), dive(x - 1, 0))),
            )
            cross = dive(x, 1)
        before, after = (ABM, ABP) if c == 1 else (AM, AP)
        ahead = plus(times(coef(before), own), times(coef(HM), cross))
        behind = minus(times(coef(after), own), times(coef(HP), cross))
        if ahead is not None:
            total = plus(total, pltpu.roll(ahead, length - 1, 1), pltpu.roll(behind, 1, 1))
        results.append(total)
    return results


def relaxed(field, first, coef, x, z):
    real = coupling(lambda i, k, c: field(i, k, c), coef, x, z)
    imag = coupling(lambda i, k, c: field(i, k, COMPS + c), coef, x, z)
    wr, wi = coef(WR), coef(WI)
    out = []
    for part in range(PARTS):
        for c in range(COMPS):
            pc = part * COMPS + c
            if part == 0:
                update = minus(times(wr, real[c]), times(wi, imag[c]))
            else:
                update = plus(times(wr, imag[c]), times(wi, real[c]))
            out.append(plus(times(1.0 - RELAX_WEIGHT, field(x, z, pc)), first(x, z, pc), update))
    return out


def scaled(fr, fi, coef):
    wr, wi = coef(WR), coef(WI)
    return wr * fr - wi * fi, wr * fi + wi * fr


def memo(fn):
    cache = {}

    def get(*key):
        if key not in cache:
            cache[key] = fn(*key)
        return cache[key]

    return get


def coef_of(coeffs, col, depth, z):
    return memo(lambda j: coeffs[pl.ds((col * COEFFS + j) * depth + z, 1), :])


def rolled_zero(x, shift):
    lane = lax.broadcasted_iota(jnp.int32, x.shape, 1)
    length = x.shape[1]
    if shift == 1:
        return jnp.where(lane == 0, 0.0, pltpu.roll(x, 1, 1))
    return jnp.where(lane == length - 1, 0.0, pltpu.roll(x, length - 1, 1))


def consts_kernel(depth, layers, table, widths, out):
    shape = (depth, out.shape[1])
    level = lax.broadcasted_iota(jnp.int32, shape, 0)
    top, bottom = widths[0, 0], widths[0, 1]
    zero = jnp.zeros(shape, jnp.int32)
    upper = jnp.maximum(top - level, 0).astype(jnp.float32) / (zero + top).astype(jnp.float32)
    lower = jnp.maximum(bottom - (depth - 1 - level), 0).astype(jnp.float32) / (
        zero + bottom
    ).astype(jnp.float32)
    out[pl.ds(0, depth), :] = SIGMA_PEAK * upper * upper + SIGMA_PEAK * lower * lower
    for row in range(3):
        for layer in range(layers):
            value = jnp.full((1, out.shape[1]), table[row, layer], jnp.float32)
            out[pl.ds(depth + row * layers + layer, 1), :] = value


def fill_coeffs(coeffs, soils, consts, depth, layers):
    shape = soils[0].shape
    sigma = consts[pl.ds(0, depth), :]
    for col, soil in enumerate(soils):
        rows = []
        for row in range(3):
            picked = jnp.zeros(shape, jnp.float32)
            for layer in range(layers):
                value = consts[pl.ds(depth + row * layers + layer, 1), :]
                picked = jnp.where(soil == layer + 1.0, value, picked)
            rows.append(picked)
        shear, lame, kappa = rows
        stiff = lame + shear
        diag_r = 6.0 * shear + 2.0 * stiff + kappa
        diag_i = kappa * sigma
        inside = soil > 0.0
        size = jnp.where(inside, diag_r * diag_r + diag_i * diag_i, 1.0)
        scale = jnp.where(inside, RELAX_WEIGHT / size, 0.0)
        both, quarter = shear + stiff, 0.25 * stiff
        values = {
            WR: scale * diag_r,
            WI: -scale * diag_i,
            A: shear,
            AB: both,
            H: quarter,
            AM: rolled_zero(shear, 1),
            ABM: rolled_zero(both, 1),
            HM: rolled_zero(quarter, 1),
            AP: rolled_zero(shear, -1),
            ABP: rolled_zero(both, -1),
            HP: rolled_zero(quarter, -1),
        }
        for j, value in values.items():
            coeffs[pl.ds((col * COEFFS + j) * depth, depth), :] = value


def tile_of(col):
    if col < HALO:
        return 0, col
    if col < HALO + WIDTH:
        return 1, col - HALO
    return 2, col - HALO - WIDTH


def pick(which, own, off, on, read):
    if which == 1:
        return read(own)
    even = lax.axis_index("tile") % 2 == 0
    first, second = read(off), read(on)
    return jnp.where(even, first, second) if which == 0 else jnp.where(even, second, first)


def slot(z, col, pc):
    return (z * COLS + col) * PC + pc


def bottom_kernel(shots, depth, layers, first_only, own, off, on, consts, start, *refs):
    bottoms, coeffs, v1, v2 = refs[:WIDTH], *refs[WIDTH:]
    work = functools.partial(
        bottom_planes, shots, depth, layers, own, off, on, consts, start, bottoms, coeffs, v1, v2
    )
    if not first_only:
        work()
        return
    slab = lax.axis_index("slab")
    pl.when(slab == 0)(work)

    @pl.when(slab != 0)
    def _():
        for ref in bottoms:
            ref[...] = jnp.zeros(ref.shape, jnp.float32)


def bottom_planes(shots, depth, layers, own, off, on, consts, start, bottoms, coeffs, v1, v2):
    at = DEEP * WIDTH * PC * shots
    soils = []
    for col in range(COLS):
        which, place = tile_of(col)
        where = pl.ds(at + place * depth, depth)
        soils.append(pick(which, own, off, on, lambda ref: ref[where, :]))
    fill_coeffs(coeffs, soils, consts, depth, layers)
    base = depth - DEEP

    def block(ref, number):
        return ref.at[pl.ds(number * shots, shots), :]

    for z in range(DEEP):
        for col in range(COLS):
            which, place = tile_of(col)
            coef = coef_of(coeffs, col, depth, base + z)
            for c in range(COMPS):
                fr, fi = (
                    pick(which, own, off, on, lambda ref: block(ref, (z * WIDTH + place) * PC + pc)[...])
                    for pc in (c, COMPS + c)
                )
                vr, vi = scaled(fr, fi, coef)
                block(v1, slot(z, col, c))[...] = vr
                block(v1, slot(z, col, COMPS + c))[...] = vi

    def first(x, z, pc):
        return block(v1, slot(z, x, pc))[...] if z < DEEP else None

    def second(x, z, pc):
        return block(v2, slot(z, x, pc))[...] if z < DEEP else None

    for z in range(1, DEEP):
        for x in range(1, COLS - 1):
            got = relaxed(memo(first), first, coef_of(coeffs, x, depth, base + z), x, z)
            for pc in range(PC):
                block(v2, slot(z, x, pc))[...] = got[pc]
    lane = lax.broadcasted_iota(jnp.int32, (shots, 2 * PATCH), 1)
    for x in range(HALO, HALO + WIDTH):
        got = relaxed(memo(second), first, coef_of(coeffs, x, depth, depth - 1), x, DEEP - 1)
        for pair in range(PC // 2):
            even, odd = got[2 * pair], got[2 * pair + 1]
            both = (
                jnp.where(lane < PATCH, even, pltpu.roll(odd, PATCH, 1)),
                jnp.where(lane < PATCH, pltpu.roll(even, PATCH, 1), odd),
            )
            for patch in range(2):
                lanes = pl.ds(pair * 2 * PATCH, 2 * PATCH)
                given = start[pl.ds(((x - HALO) * 2 + patch) * shots, shots), lanes]
                bottoms[x - HALO][pl.ds(patch * shots, shots), lanes] = both[patch] + given


def full_kernel(shots, depth, coeffs, low, low_on, low_off, high, high_off, high_on, out, v1, v2):
    stride = PC * WIDTH * depth
    lows, highs = (low, low_off, low_on), (high, high_off, high_on)
    plane = COLS * PC * shots

    def at(z, col, pc):
        return pl.ds(pl.multiple_of((z + 1) * plane + (col * PC + pc) * shots, shots), shots)

    for ref in (v1, v2):
        for z in (-1, depth):
            for n in range(COLS * PC):
                ref[pl.ds((z + 1) * plane + n * shots, shots), :] = jnp.zeros((shots, 2 * PATCH), jnp.float32)

    def begin(tiles, shift):
        def run(z, carry):
            for col in range(COLS):
                which, place = tile_of(col)
                coef = coef_of(coeffs, col, depth, z)
                for c in range(COMPS):
                    number = ((z - shift) * WIDTH + place) * PC + c
                    fr, fi = (
                        pick(which, *tiles, lambda ref: ref[pl.ds(pl.multiple_of(n * shots, shots), shots), :])
                        for n in (number, number + COMPS)
                    )
                    vr, vi = scaled(fr, fi, coef)
                    v1[at(z, col, c), :] = vr
                    v1[at(z, col, COMPS + c), :] = vi
            return carry

        return run

    lax.fori_loop(0, depth - DEEP, begin(lows, 0), 0)
    lax.fori_loop(depth - DEEP, depth, begin(highs, depth - DEEP), 0)

    def first(x, z, pc):
        return v1[at(z, x, pc), :]

    def second(x, z, pc):
        return v2[at(z, x, pc), :]

    def middle(z, carry):
        for x in range(1, COLS - 1):
            got = relaxed(first, first, coef_of(coeffs, x, depth, z), x, z)
            for pc in range(PC):
                v2[at(z, x, pc), :] = got[pc]
        return carry

    lax.fori_loop(0, depth, middle, 0)

    def last(z, carry):
        for x in range(HALO, HALO + WIDTH):
            got = relaxed(second, first, coef_of(coeffs, x, depth, z), x, z)
            for pc in range(PC):
                out[pl.ds((pc * WIDTH + x - HALO) * depth + z, shots, stride=stride), :] = got[pc]
        return carry

    lax.fori_loop(0, depth, last, 0)


def inject_kernel(shots, depth, offs, coeffs, base, *refs):
    own, traces, halos = refs[:WIDTH], refs[WIDTH : 2 * WIDTH], refs[2 * WIDTH : -4]
    out, whole, v1, v2 = refs[-4:]
    for col, trace in enumerate(traces):
        whole[pl.ds(col * trace.shape[0], trace.shape[0]), :] = trace[...]
    off, on = halos[:offs], halos[offs:]
    stride = PC * WIDTH * depth

    def block(ref, number):
        return ref.at[pl.ds(number * shots, shots), :]

    lane = lax.broadcasted_iota(jnp.int32, (shots, 2 * PATCH), 1)
    for col in range(COLS):
        which, place = tile_of(col)
        coef = coef_of(coeffs, col, depth, 0)
        planes = []
        for pair in range(PC // 2):
            halves = []
            for patch in range(2):
                where = (
                    pl.ds((place * 2 + patch) * shots, shots),
                    pl.ds(pair * 2 * PATCH, 2 * PATCH),
                )
                if which == 1:
                    halves.append(own[place][pl.ds(patch * shots, shots), where[1]])
                else:
                    halves.append(
                        pick(which, None, off, on, lambda refs: plus(*[ref[where] for ref in refs]))
                    )
            planes.append(jnp.where(lane < PATCH, halves[0], pltpu.roll(halves[1], PATCH, 1)))
            planes.append(jnp.where(lane < PATCH, pltpu.roll(halves[0], PATCH, 1), halves[1]))
        shear = coef(A)
        for c in range(COMPS):
            vr, vi = scaled(shear * planes[c], shear * planes[COMPS + c], coef)
            block(v1, slot(0, col, c))[...] = vr
            block(v1, slot(0, col, COMPS + c))[...] = vi

    def first(x, z, pc):
        return block(v1, slot(0, x, pc))[...] if z == 0 else None

    def second(x, z, pc):
        return block(v2, slot(z, x, pc))[...] if 0 <= z < 2 else None

    for z in range(2):
        for x in range(1, COLS - 1):
            got = relaxed(memo(first), first, coef_of(coeffs, x, depth, z), x, z)
            for pc in range(PC):
                block(v2, slot(z, x, pc))[...] = got[pc]
    out[...] = base[...]
    for z in range(3):
        for x in range(HALO, HALO + WIDTH):
            got = relaxed(memo(second), first, coef_of(coeffs, x, depth, z), x, z)
            for pc in range(PC):
                where = (pl.ds((pc * WIDTH + x - HALO) * depth + z, shots, stride=stride), slice(None))
                out[where] = base[where] + got[pc]


def split_kernel(blocks, high, low):
    whole = blocks[...]
    top = whole.astype(jnp.bfloat16)
    high[...] = top
    low[...] = (whole - top.astype(jnp.float32)).astype(jnp.bfloat16)


def product(shots, x, high, low, add, out, first):
    size = x.shape[1]
    for chain in range(x.shape[0] // shots):
        rows = pl.ds(chain * shots, shots)
        whole = x[rows, :]
        top = whole.astype(jnp.bfloat16)
        rest = (whole - top.astype(jnp.float32)).astype(jnp.bfloat16)
        block = pl.ds((first + chain) * size, size)
        wide = jnp.dot(
            jnp.concatenate([top, rest], axis=0), high[block, :], preferred_element_type=jnp.float32
        )
        thin = jnp.dot(top, low[block, :], preferred_element_type=jnp.float32)
        total = wide[:shots] + wide[shots:] + thin
        out[rows, :] = total if add is None else total + add[rows, :]


def start_kernel(shots, inflow, high, low, out, *helds):
    slab = lax.axis_index("slab")

    @pl.when(slab == 0)
    def _():
        product(shots, inflow, high, low, None, out, 0)

    @pl.when(slab != 0)
    def _():
        out[...] = jnp.zeros(out.shape, jnp.float32)

    for col, ref in enumerate(helds):
        ref[...] = inflow[pl.ds(col * ref.shape[0], ref.shape[0]), :]


def hop_kernel(shots, turn, col, groups, *refs):
    arrived, high, low, bottom, trace, held, *rest = refs
    sides, (new_trace, new_held, *sums) = rest[: sum(groups)], rest[sum(groups) :]
    slab = lax.axis_index("slab")

    @pl.when(slab == turn)
    def _():
        product(shots, arrived, high, low, bottom, new_trace, col * (arrived.shape[0] // shots))
        new_held[...] = arrived[...]

    @pl.when(slab != turn)
    def _():
        new_trace[...] = trace[...]
        new_held[...] = held[...]

    for ref, count in zip(sums, [g for g in groups if g]):
        ref[...] = plus(*[side[...] for side in sides[:count]])
        sides = sides[count:]


def gather_kernel(turn, *refs):
    mine, rows = refs[-1], refs[0].shape[0]
    traces, helds = refs[:WIDTH], refs[WIDTH:-1]

    def fill(parts):
        for number, part in enumerate(parts):
            mine[pl.ds(number * rows, rows), :] = part[...]

    slab = lax.axis_index("slab")
    pl.when(slab == turn)(lambda: fill(traces))
    pl.when(slab != turn)(lambda: fill(helds))


def per_device(source, soil_index, soil_table, pml_width, interface_blocks, inflow):
    shots, _, _, width, depth, length = source.shape
    layers = soil_table.shape[1]
    size = interface_blocks.shape[-1]
    slabs, tiles = lax.axis_size("slab"), lax.axis_size("tile")
    f32, bf16 = jnp.float32, jnp.bfloat16
    chains = width * (length // PATCH)
    low_rows = (depth - DEEP) * width * PC * shots
    high_rows = DEEP * width * PC * shots + width * depth

    off = [p for t in range(1, tiles - 1, 2) for p in ((t, t + 1), (t + 1, t))]
    on = [p for t in range(0, tiles - 1, 2) for p in ((t, t + 1), (t + 1, t))]

    def pairs(slab_moves, tile_moves):
        return [(a * tiles + t, b * tiles + u) for a, b in slab_moves for t, u in tile_moves]

    def both(x, moves):
        return lax.ppermute(x, ("slab", "tile"), moves)

    src, soil = source.reshape(-1, length), soil_index.reshape(-1, length)
    (high,) = call(
        "pack_high",
        functools.partial(pack_high_kernel, shots, depth),
        [((high_rows, length), f32)],
        [pltpu.with_memory_space_constraint(x, pltpu.HBM) for x in (src, soil)],
        [ANY, ANY],
        [
            pltpu.VMEM(src.shape, f32),
            pltpu.VMEM(soil.shape, jnp.int32),
            pltpu.SemaphoreType.DMA((2,)),
        ],
    )
    high_off, high_on = lax.ppermute(high, "tile", off), lax.ppermute(high, "tile", on)

    blocks = interface_blocks.reshape(chains * size, size)
    heavy, light = call("split", split_kernel, [(blocks.shape, bf16)] * 2, [blocks])
    held = inflow.reshape(chains * shots, size)
    row_shape = ((chains * shots, size), f32)
    chunk = (chains // width * shots, size)
    start, *helds = call(
        "start",
        functools.partial(start_kernel, shots),
        [row_shape] + [(chunk, f32)] * width,
        [held, heavy, light],
    )
    table_shape = (COLS * COEFFS * depth, length)
    planes = [pltpu.VMEM((DEEP * COLS * PC * shots, length), f32)] * 2
    (consts,) = call(
        "consts",
        functools.partial(consts_kernel, depth, layers),
        [((depth + 3 * layers, length), f32)],
        [soil_table, pml_width],
        [SMEM, SMEM],
    )
    near = [high, high_off, high_on, consts, start]
    traces = call(
        "first",
        functools.partial(bottom_kernel, shots, depth, layers, True),
        [(chunk, f32)] * width,
        near,
        None,
        [pltpu.VMEM(table_shape, f32)] + planes,
    )
    *bottoms, coeffs = call(
        "bottom",
        functools.partial(bottom_kernel, shots, depth, layers, False),
        [(chunk, f32)] * width + [(table_shape, f32)],
        near,
        None,
        planes,
        flops=HOP_COST,
    )
    offs, ons = [], []
    first_far, mine = slabs // 2, None
    for hop in range(slabs - 1):
        step = pairs([(hop, hop + 1)], [(t, t) for t in range(tiles)])
        arrived = [both(trace, step) for trace in traces]
        groups = (len(offs), len(ons))
        sides = [*offs, *ons]
        if hop in (2, slabs - 2):
            arrived = lax.optimization_barrier(arrived)
        from_off, from_on = [], []
        if hop >= first_far:
            same = range(hop) if hop == first_far else [first_far] if hop == first_far + 1 else []
            from_off = [both(mine, pairs([(hop, hop + 1)] + [(s, s) for s in same], off))]
        if hop == slabs - 2:
            (entered,) = call(
                "entered",
                functools.partial(gather_kernel, hop + 1),
                [row_shape],
                [*arrived, *helds],
                flops=GATHER_COST,
            )
            from_on = [lax.ppermute(entered, "tile", on)]
        if hop == 2:
            again, _ = lax.optimization_barrier((src, traces))
            (low,) = call(
                "pack_low",
                functools.partial(pack_low_kernel, shots, depth),
                [((low_rows, length), f32)],
                [again],
                flops=LOW_COST,
            )
            low_off, low_on = lax.ppermute(low, "tile", off), lax.ppermute(low, "tile", on)
        if hop == first_far:
            lows, _ = lax.optimization_barrier(((low, low_on, low_off), traces))
            (solved,) = call(
                "full",
                functools.partial(full_kernel, shots, depth),
                [((shots * PC * width * depth, length), f32)],
                [coeffs, *lows, high, high_off, high_on],
                None,
                [pltpu.VMEM(((depth + 2) * COLS * PC * shots, length), f32)] * 2,
                flops=FULL_COST,
                limit=12 * MIB,
            )
            arrived[-1], solved = lax.optimization_barrier((arrived[-1], solved))
        sums = []
        new_traces, new_helds = [None] * width, [None] * width
        for col in reversed(range(width)):
            if hop == first_far and col < width - 1:
                arrived[col], _ = lax.optimization_barrier((arrived[col], new_traces[-1]))
            counts = groups if col == width - 1 else (0, 0)
            new_traces[col], new_helds[col], *more = call(
                f"hop{hop}_{col}",
                functools.partial(hop_kernel, shots, hop + 1, col, counts),
                [(chunk, f32)] * 2 + [row_shape] * sum(c > 0 for c in counts),
                [arrived[col], heavy, light, bottoms[col], traces[col], helds[col]]
                + (sides if col == width - 1 else []),
                flops=HOP_COSTS[hop],
            )
            sums = more or sums
        traces, helds = new_traces, new_helds
        if first_far - 1 <= hop < slabs - 2:
            (mine,) = call(
                f"gather{hop}",
                functools.partial(gather_kernel, hop + 1),
                [row_shape],
                [*traces, *helds],
                flops=GATHER_COST,
            )
        offs = ([sums.pop(0)] if groups[0] else []) + from_off
        ons = ([sums.pop(0)] if groups[1] else []) + from_on
    result, whole = call(
        "inject",
        functools.partial(inject_kernel, shots, depth, len(offs)),
        [(solved.shape, f32), row_shape],
        [coeffs, solved, *helds, *traces, *offs, *ons],
        None,
        planes,
    )
    traces = whole.reshape(width, 1, length // PATCH, shots, size)
    return result.reshape(source.shape), traces


def solution(mesh):
    in_specs = (
        P(None, None, None, "tile", "slab", None),
        P("tile", "slab", None),
        P(),
        P("slab", None),
        P("tile", "slab", None, None, None),
        P("tile", None, None, None),
    )
    out_specs = (P(None, None, None, "tile", "slab", None), P("tile", "slab", None, None, None))
    return jax.shard_map(
        per_device, mesh=mesh, in_specs=in_specs, out_specs=out_specs, check_vma=False
    )
```
